32 devices in a mesh: sub: 8 (over z, x), inner: 4 (over y, core).
Axes of the slice: x: 2, y: 2, z: 4, core: 2. Of those that a mesh axis runs over, the one named last changes fastest.
Arguments:
- operator_tiles: float32 [128, 27, 64, 64], P(('sub', 'inner')), may hold values from -0.15625 to 0.15625
- operator_cols: int32 [128, 27], P(('sub', 'inner')), may hold values from 0 to 11, as said below
- operator_count: int32 [128], P(('sub', 'inner')), may hold values from 13 to 27
- prolong_tiles: float32 [128, 3, 64, 64], P(('sub', 'inner')), may hold values from -0.75 to 0.75
- prolong_cols: int32 [128, 3], P(('sub', 'inner')), may hold values from 0 to 31, as said below
- prolong_count: int32 [128], P(('sub', 'inner')), may hold values from 1 to 3
- fetch_rows: int32 [64, 1], P(('sub', 'inner')), may hold values from 0 to 3, as said below
Outputs:
- coarse_matrix: float32 [32, 12, 64, 64], P('sub')
The draws below stay inside these ranges and needn't reach their ends.
Inputs may be any that keep to these rules, and one draw needn't show every extreme that they name: `operator_cols`: each entry is a local block row (below 4) or a ghost slot; slot 4 + j + p is position p of the upward list of inner device j of the group below, slot 4 + (4 + j) + p position p of the downward list of inner device j of the group above; only existing groups are named. Entry 0 of each row is the row itself. `fetch_rows`: row 2 d lists the distinct local rows that device d sends to the group below, starting with row 0; row 2 d + 1 those it sends to the group above, starting with row 3. `prolong_cols`: A block row of group s names distinct coarse blocks of its own group, s * 4 to (s + 1) * 4 - 1.
All inputs are finite; a program needn't handle non-finite values.
Results may differ from the reference program's by a relative error of at most 0.0003.
Values sent between devices are 32-bit elements; how exact they have to be, the bound alone decides.
No kernel may reach another device: no remote copies, remote signals or barrier semaphores. Data moves between devices by JAX's collectives and lax.ppermute only.
A program may use at most 64 MiB of HBM per device.

```python
import jax
import jax.numpy as jnp
from jax import lax

B = 64
BR = 4
KA = 27
KP = 3
CG = 4
SEND = 1
NFB = 128
NCB = 32
N_SUB = 8
N_INNER = 4


def draw_fetch_rows(key, part):
    key = jax.random.fold_in(key, 11)
    list_total = 2 * N_SUB * N_INNER
    key_list = jax.random.split(key, list_total)

    def one_list(sub_key, flag):
        scores = jax.random.randint(sub_key, (BR - 1,), 0, 1 << 20) * (BR - 1) + jnp.arange(BR - 1, dtype=jnp.int32)
        ordering = jnp.argsort(scores, stable=True).astype(jnp.int32)
        others = ordering[:SEND - 1] + jnp.where(flag == 0, 1, 0)
        leading = jnp.where(flag == 0, 0, BR - 1).astype(jnp.int32)
        return jnp.concatenate([leading[None], others.astype(jnp.int32)])
    flags = (jnp.arange(list_total, dtype=jnp.int32) % 2).astype(jnp.int32)
    return jax.vmap(one_list)(key_list, flags).astype(jnp.int32)


def draw_operator_cols(key, part):
    key = jax.random.fold_in(key, 12)
    row_total = BR * N_SUB * N_INNER
    row_ids = jnp.arange(row_total, dtype=jnp.int32)
    device = row_ids // BR
    group = device // N_INNER
    local_row = row_ids % BR
    span = N_INNER * SEND
    key_kind, key_side, key_local, key_ghost = jax.random.split(key, 4)
    kind = jax.random.randint(key_kind, (row_total, KA), 0, 2)
    side = jax.random.randint(key_side, (row_total, KA), 0, 2)
    side = jnp.where(group[:, None] == 0, 1, side)
    side = jnp.where(group[:, None] == N_SUB - 1, 0, side)
    local_pick = jax.random.randint(key_local, (row_total, KA), 0, BR)
    ghost_pick = BR + side * span + jax.random.randint(key_ghost, (row_total, KA), 0, span)
    entries = jnp.where(kind == 0, local_pick, ghost_pick).astype(jnp.int32)
    entries = entries.at[:, 0].set(local_row)
    forced = (local_row == BR - 1) & (group < N_SUB - 1)
    entries = entries.at[:, 1].set(jnp.where(forced, BR + 2 * span - 1, entries[:, 1]))
    return entries.astype(jnp.int32)


def draw_prolong_cols(key, part):
    key = jax.random.fold_in(key, 13)
    row_total = BR * N_SUB * N_INNER
    row_ids = jnp.arange(row_total, dtype=jnp.int32)
    group = row_ids // (BR * N_INNER)
    scores = jax.random.randint(key, (row_total, CG), 0, 1 << 20) * CG + jnp.arange(CG, dtype=jnp.int32)[None, :]
    ordering = jnp.argsort(scores, axis=1, stable=True).astype(jnp.int32)
    return (group[:, None] * CG + ordering[:, :KP]).astype(jnp.int32)


def plant(values, rng, smallest, high):
    longest = values.shape.index(max(values.shape))
    spots = []
    for shift in (0, 1):
        where = [jax.random.randint(jax.random.fold_in(rng, axis), (), 0, length) for axis, length in enumerate(values.shape)]
        where[longest] = (where[longest] + shift) % values.shape[longest]
        spots.append(tuple(where))
    return values.at[spots[0]].set(smallest).at[spots[1]].set(high)


def block_levels(rng, dims, cuts, least, largest):
    loudness = 1.0
    for dim, blocks in cuts:
        draws = jax.random.uniform(jax.random.fold_in(jax.random.fold_in(rng, 6), dim), (blocks,), jnp.float32, least / len(cuts), largest / len(cuts))
        loudness = loudness * jnp.repeat(jnp.exp(draws), dims[dim] // blocks).reshape((-1,) + (1,) * (len(dims) - 1 - dim))
    return loudness


def noise(own_key, shape, spread, bound, cuts=(), held_as=jnp.bfloat16):
    result = spread * jax.random.normal(own_key, shape, jnp.float32)
    if cuts:
        result = result * block_levels(own_key, shape, cuts, -0.22, 0.18)
    return jnp.clip(result, -bound, bound).astype(held_as)


def setup_inputs(seed: int = 0) -> dict:
    streams_of = jax.random.split(jax.random.key(seed), 8)
    return {
        "operator_tiles": noise(streams_of[0], (NFB, KA, B, B), (B * KA) ** -0.5, 0.15625, ((0, 32),), jnp.float32),
        "operator_cols": draw_operator_cols(jax.random.fold_in(streams_of[7], 71), 0),
        "operator_count": plant(jax.random.randint(streams_of[2], (NFB,), KA // 2, KA + 1), jax.random.fold_in(streams_of[2], 1), KA // 2, KA).astype(jnp.int32),
        "prolong_tiles": noise(streams_of[3], (NFB, KP, B, B), B ** -0.5, 0.75, ((0, 32),), jnp.float32),
        "prolong_cols": draw_prolong_cols(jax.random.fold_in(streams_of[7], 71), 0),
        "prolong_count": plant(jax.random.randint(streams_of[5], (NFB,), 1, KP + 1), jax.random.fold_in(streams_of[5], 1), 1, KP).astype(jnp.int32),
        "fetch_rows": draw_fetch_rows(jax.random.fold_in(streams_of[7], 71), 0),
    }


def dense_prolongator(prolong_tiles, prolong_cols, prolong_count):
    row_total = prolong_tiles.shape[0]
    group_of = (jnp.arange(row_total, dtype=jnp.int32) // (BR * N_INNER)).astype(jnp.int32)
    local_cols = prolong_cols - group_of[:, None] * CG
    tile_keep = (jnp.arange(KP, dtype=jnp.int32)[None, :] < prolong_count[:, None]).astype(jnp.float32)
    placed = (local_cols[:, :, None] == jnp.arange(CG, dtype=jnp.int32)[None, None, :]).astype(jnp.float32)
    placed = placed * tile_keep[:, :, None]
    return jnp.einsum("img,imbc->igbc", placed, prolong_tiles, precision=lax.Precision.HIGHEST)


def reference(operator_tiles, operator_cols, operator_count, prolong_tiles, prolong_cols, prolong_count, fetch_rows):
    dense_all = dense_prolongator(prolong_tiles, prolong_cols, prolong_count)
    span = N_INNER * SEND
    device_total = N_SUB * N_INNER

    def device_part(device):
        group = device // N_INNER
        start = (device * BR).astype(jnp.int32)
        columns = lax.dynamic_slice_in_dim(operator_cols, start, BR, 0)
        tiles = lax.dynamic_slice_in_dim(operator_tiles, start, BR, 0)
        counts = lax.dynamic_slice_in_dim(operator_count, start, BR, 0)
        ghost = columns - BR
        side = jnp.where(ghost < span, 0, 1)
        within = jnp.where(side == 0, ghost, ghost - span)
        peer = within // SEND
        position = jnp.clip(within % SEND, 0, SEND - 1)
        source_group = jnp.where(side == 0, group - 1, group + 1)
        source = jnp.clip(source_group * N_INNER + peer, 0, device_total - 1)
        list_row = jnp.clip(2 * source + jnp.where(side == 0, 1, 0), 0, 2 * device_total - 1)
        fetched = fetch_rows[list_row, position]
        global_row = jnp.where(columns < BR, start + columns, source * BR + fetched).astype(jnp.int32)
        region = jnp.where(columns < BR, 1, jnp.where(side == 0, 0, 2))
        pieces = dense_all[global_row]
        products = jnp.einsum("ikbc,ikgcd->ikgbd", tiles, pieces, precision=lax.Precision.HIGHEST)
        live_mask = (jnp.arange(KA, dtype=jnp.int32)[None, :] < counts[:, None]).astype(jnp.float32)
        weights = (region[:, :, None] == jnp.arange(3, dtype=jnp.int32)[None, None, :]).astype(jnp.float32)
        weights = weights * live_mask[:, :, None]
        applied = jnp.einsum("ikq,ikgbd->iqgbd", weights, products, precision=lax.Precision.HIGHEST)
        own_rows = lax.dynamic_slice_in_dim(dense_all, start, BR, 0)
        return jnp.einsum("igcb,iqhcd->gqhbd", own_rows, applied, precision=lax.Precision.HIGHEST)

    def group_part(group):
        def add_device(member, total):
            return total + device_part(group * N_INNER + member)

        start_total = jnp.zeros((CG, 3, CG, B, B), jnp.float32)
        summed = lax.fori_loop(0, N_INNER, add_device, start_total)
        return summed.reshape(CG, 3 * CG, B, B)

    stacked = lax.map(group_part, jnp.arange(N_SUB, dtype=jnp.int32))
    return stacked.reshape(NCB, 3 * CG, B, B)
```

```python
import functools

import jax
import jax.numpy as jnp
from jax import lax
from jax.experimental import pallas as pl
from jax.experimental.pallas import tpu as pltpu
from jax.sharding import PartitionSpec as P

CG = 4
CORES = 2
VMEM_BYTES = 32 * 1024 * 1024


def halves(value):
    high = value.astype(jnp.bfloat16)
    low = (value - high.astype(jnp.float32)).astype(jnp.bfloat16)
    return high, low


def product(left, right):
    left_high, left_low = halves(left)
    right_high, right_low = halves(right)
    dot = functools.partial(jnp.dot, preferred_element_type=jnp.float32)
    return dot(left_high, right_high) + (dot(left_low, right_high) + dot(left_high, right_low))


def left_kernel(
    cols_ref,
    count_ref,
    prolong_cols_ref,
    prolong_count_ref,
    fetch_ref,
    place_ref,
    tiles_hbm,
    prolong_hbm,
    mine_ref,
    send_ref,
    straight_ref,
    crossed_ref,
    dense_ref,
    local_ref,
    tiles,
    prolong,
    slots,
    tile_sems,
    prolong_sem,
):
    rows, entries, size, _ = tiles.shape
    fetched = mine_ref.shape[1] // size
    prolong_copy = pltpu.make_async_copy(prolong_hbm, prolong, prolong_sem)
    prolong_copy.start()
    copies = [
        pltpu.make_async_copy(tiles_hbm.at[row], tiles.at[row], tile_sems.at[row])
        for row in range(rows)
    ]
    for copy in copies:
        copy.start()
    slots[...] = jnp.zeros_like(slots)
    first_coarse = place_ref[0] * CG
    core = place_ref[1]

    prolong_copy.wait()
    for row in range(rows):
        blocks = []
        for coarse in range(CG):
            block = None
            for m in range(prolong.shape[1]):
                hit = (prolong_cols_ref[row, m] == first_coarse + coarse) & (
                    m < prolong_count_ref[row]
                )
                term = prolong[row, m] * jnp.where(hit, 1.0, 0.0)
                block = term if block is None else block + term
            blocks.append(block)
        dense_ref[row * size : (row + 1) * size, :] = jnp.concatenate(blocks, axis=1)

    for target, ref in ((core, straight_ref), (1 - core, crossed_ref)):
        taken = pl.multiple_of(fetch_ref[1 - target, 0] * size, size)
        ref[...] = dense_ref[pl.ds(taken, size), :]

    for row in range(rows):
        copies[row].wait()
        for entry in range(entries):
            col = cols_ref[row, entry]
            ghost = col - rows
            above = ghost >= fetched
            within = jnp.where(above, ghost - fetched, ghost)
            is_mine = above == (core == 1)
            slot = jnp.where(col < rows, col, rows + jnp.where(is_mine, within, fetched + within))
            slot = jnp.where(entry < count_ref[row], slot, rows + 2 * fetched)
            slots[row, slot] += tiles[row, entry]

    def gathered(first, count):
        return jnp.concatenate(
            [
                jnp.concatenate([slots[row, first + j] for j in range(count)], axis=1)
                for row in range(rows)
            ],
            axis=0,
        )

    turned = dense_ref[...].T
    mine_ref[...] = product(turned, gathered(rows, fetched))
    send_ref[...] = product(turned, gathered(rows + fetched, fetched))
    local_ref[...] = gathered(0, rows)


def middle_kernel(place_ref, dense_ref, local_ref, mine_ref, send_ref, whole):
    core = place_ref[1]
    dense = dense_ref[...]
    whole[...] = product(product(dense.T, local_ref[...]), dense)
    half = mine_ref.shape[0]
    mine_ref[...] = whole[pl.ds(pl.multiple_of(core * half, half), half), :]
    send_ref[...] = whole[pl.ds(pl.multiple_of((1 - core) * half, half), half), :]


def window_kernel(place_ref, held_ref, came_ref, *refs):
    ghosts, result_ref, prolong = refs[:-2], refs[-2], refs[-1]
    core, chip = place_ref[1], place_ref[2]
    size = ghosts[0].shape[0]
    chips = len(ghosts) // CORES
    for index, ghost in enumerate(ghosts):
        shift, cross = divmod(index, CORES)
        source = lax.rem(chip + shift, chips) * CORES + lax.rem(core + cross, CORES)
        prolong[pl.ds(pl.multiple_of(source * size, size), size), :] = ghost[...]
    result_ref[...] = product(held_ref[...] + came_ref[...], prolong[...])


def write_blocks(out_ref, first, value):
    size = out_ref.shape[-1]
    for g in range(value.shape[0] // size):
        for h in range(value.shape[1] // size):
            out_ref[g, first + h] = value[g * size : (g + 1) * size, h * size : (h + 1) * size]


def outer_kernel(place_ref, own_ref, other_ref, out_ref):
    core = place_ref[1]
    write_blocks(out_ref, 2 * CG * core, own_ref[...])
    write_blocks(out_ref, 2 * CG * (1 - core), other_ref[...])


def inner_kernel(place_ref, held_ref, came_ref, far_held_ref, far_came_ref, _, out_ref, whole):
    core = place_ref[1]
    half = held_ref.shape[0]
    whole[pl.ds(pl.multiple_of(core * half, half), half), :] = held_ref[...] + came_ref[...]
    whole[pl.ds(pl.multiple_of((1 - core) * half, half), half), :] = (
        far_held_ref[...] + far_came_ref[...]
    )
    write_blocks(out_ref, 0, whole[...])


SMEM = pl.BlockSpec(memory_space=pltpu.SMEM)
VMEM = pl.BlockSpec(memory_space=pltpu.VMEM)
ANY = pl.BlockSpec(memory_space=pl.ANY)
PARAMS = pltpu.CompilerParams(vmem_limit_bytes=VMEM_BYTES)


def f32(*shape):
    return jax.ShapeDtypeStruct(shape, jnp.float32)


def per_device(
    operator_tiles,
    operator_cols,
    operator_count,
    prolong_tiles,
    prolong_cols,
    prolong_count,
    fetch_rows,
):
    rows, entries, size, _ = operator_tiles.shape
    subs, fetched = lax.axis_size("sub"), lax.axis_size("inner")
    chips = fetched // CORES
    width = CG * size
    position = lax.axis_index("inner")
    place = jnp.stack(
        [lax.axis_index("sub"), lax.rem(position, CORES), lax.div(position, CORES)]
    ).astype(jnp.int32)

    held, send, straight, crossed, dense, local = pl.pallas_call(
        left_kernel,
        out_shape=[
            f32(width, fetched * size),
            f32(width, fetched * size),
            f32(size, width),
            f32(size, width),
            f32(rows * size, width),
            f32(rows * size, rows * size),
        ],
        in_specs=[SMEM] * 6 + [ANY] * 2,
        out_specs=[VMEM] * 6,
        scratch_shapes=[
            pltpu.VMEM(operator_tiles.shape, jnp.float32),
            pltpu.VMEM(prolong_tiles.shape, jnp.float32),
            pltpu.VMEM((rows, rows + 2 * fetched + 1, size, size), jnp.float32),
            pltpu.SemaphoreType.DMA((rows,)),
            pltpu.SemaphoreType.DMA,
        ],
        compiler_params=PARAMS,
        name="left",
    )(
        operator_cols,
        operator_count,
        prolong_cols,
        prolong_count,
        fetch_rows,
        place,
        operator_tiles,
        prolong_tiles,
    )

    swap_cores = [(i, i ^ 1) for i in range(fetched)]
    both = ("sub", "inner")

    def other_core(value):
        return lax.ppermute(value, "inner", swap_cores)

    def chip_sum(value):
        step = 1
        while step < chips:
            came = lax.ppermute(
                value, "inner", [(i, i ^ (step * CORES)) for i in range(fetched)]
            )
            step *= 2
            if step < chips:
                value = value + came
        return value, came

    ghosts = []
    for shift in range(chips):
        for cross in range(CORES):
            pairs = []
            for sub in range(subs):
                for chip in range(chips):
                    for core in range(CORES):
                        source_sub = sub - 1 if core == 0 else sub + 1
                        if 0 <= source_sub < subs:
                            source = (chip + shift) % chips * CORES + (core + cross) % CORES
                            pairs.append(
                                (source_sub * fetched + source, sub * fetched + chip * CORES + core)
                            )
            ghosts.append(lax.ppermute(crossed if cross else straight, both, pairs))

    middle_held, middle_send = pl.pallas_call(
        middle_kernel,
        out_shape=[f32(width // CORES, width)] * 2,
        in_specs=[SMEM, VMEM, VMEM],
        out_specs=[VMEM] * 2,
        scratch_shapes=[pltpu.VMEM((width, width), jnp.float32)],
        compiler_params=PARAMS,
        name="middle",
    )(place, dense, local)

    held, came = chip_sum(held + other_core(send))
    middle_held, middle_came = chip_sum(middle_held + other_core(middle_send))

    window = pl.pallas_call(
        window_kernel,
        out_shape=f32(width, width),
        in_specs=[SMEM] + [VMEM] * (2 + len(ghosts)),
        out_specs=VMEM,
        scratch_shapes=[pltpu.VMEM((fetched * size, width), jnp.float32)],
        compiler_params=PARAMS,
        name="window",
    )(place, held, came, *ghosts)

    out_shape = f32(CG, 3 * CG, size, size)
    outer = pl.pallas_call(
        outer_kernel,
        out_shape=out_shape,
        in_specs=[SMEM] + [VMEM] * 2,
        out_specs=VMEM,
        compiler_params=PARAMS,
        name="outer",
    )(place, window, other_core(window))

    def whole_block(*shape):
        return pl.BlockSpec(shape, lambda step: (0,) * len(shape))

    half_block = whole_block(width // CORES, width)
    return pl.pallas_call(
        inner_kernel,
        grid=(1,),
        out_shape=out_shape,
        in_specs=[SMEM] + [half_block] * 4 + [ANY],
        out_specs=pl.BlockSpec((CG, CG, size, size), lambda step: (0, 1, 0, 0)),
        scratch_shapes=[pltpu.VMEM((width, width), jnp.float32)],
        input_output_aliases={5: 0},
        compiler_params=PARAMS,
        name="inner",
    )(
        place,
        middle_held,
        middle_came,
        other_core(middle_held),
        other_core(middle_came),
        outer,
    )


def solution(mesh):
    placed = (
        P(("sub", "inner"), None, None, None),
        P(("sub", "inner"), None),
        P(("sub", "inner")),
        P(("sub", "inner"), None, None, None),
        P(("sub", "inner"), None),
        P(("sub", "inner")),
        P(("sub", "inner"), None),
    )
    return jax.shard_map(
        per_device,
        mesh=mesh,
        in_specs=placed,
        out_specs=P("sub", None, None, None),
        check_vma=False,
    )
```

```python
import functools

import jax
import jax.numpy as jnp
from jax import lax
from jax.experimental import pallas as pl
from jax.experimental.pallas import tpu as pltpu
from jax.sharding import PartitionSpec as P

CG = 4
CORES = 2
VMEM_BYTES = 32 * 1024 * 1024


def split(value):
    high = value.astype(jnp.bfloat16)
    low = (value - high.astype(jnp.float32)).astype(jnp.bfloat16)
    return high, low


def product(left, right):
    dot = functools.partial(jnp.dot, preferred_element_type=jnp.float32)
    return dot(left[0], right[0]) + (dot(left[1], right[0]) + dot(left[0], right[1]))


def left_kernel(
    cols_hbm,
    count_hbm,
    prolong_cols_hbm,
    prolong_count_hbm,
    fetch_hbm,
    tiles_hbm,
    prolong_hbm,
    keep_outer_ref,
    send_outer_ref,
    keep_inner_ref,
    send_inner_ref,
    straight_ref,
    cols,
    count,
    prolong_cols,
    prolong_count,
    fetch,
    tiles,
    prolong,
    dense,
    whole,
    *rest,
):
    slots, (tile_sems, small_sems) = rest[:-2], rest[-2:]
    rows, entries, size, _ = tiles.shape
    fetched = keep_outer_ref.shape[1] // size
    smalls = [
        pltpu.make_async_copy(source, target, small_sems.at[index])
        for index, (source, target) in enumerate(
            (
                (prolong_cols_hbm, prolong_cols),
                (prolong_count_hbm, prolong_count),
                (fetch_hbm, fetch),
                (cols_hbm, cols),
                (count_hbm, count),
                (prolong_hbm, prolong),
            )
        )
    ]
    copies = [
        pltpu.make_async_copy(tiles_hbm.at[row], tiles.at[row], tile_sems.at[row])
        for row in range(rows)
    ]
    for copy in smalls + copies:
        copy.start()
    for ref in slots:
        ref[...] = jnp.zeros_like(ref)
    first_coarse = lax.axis_index("sub") * CG
    core = lax.rem(lax.axis_index("inner"), CORES)
    for copy in smalls:
        copy.wait()

    for row in range(rows):
        blocks = []
        for coarse in range(CG):
            block = None
            for m in range(prolong.shape[1]):
                hit = (prolong_cols[row, m] == first_coarse + coarse) & (m < prolong_count[row])
                term = prolong[row, m] * jnp.where(hit, 1.0, 0.0)
                block = term if block is None else block + term
            blocks.append(block)
        dense[row * size : (row + 1) * size, :] = jnp.concatenate(blocks, axis=1)

    half = keep_inner_ref.shape[0]
    straight_ref[...] = dense[pl.ds(pl.multiple_of(fetch[1 - core] * size, size), size), :]
    send_inner_ref[half:, :] = dense[pl.ds(pl.multiple_of(fetch[core] * size, size), size), :]

    for first in range(0, rows, 2):
        pair = range(first, min(first + 2, rows))
        for row in pair:
            copies[row].wait()
        for entry in range(entries):
            for row in pair:
                slot = jnp.where(entry < count[row], cols[row, entry], rows + 2 * fetched)
                slots[row][slot] += tiles[row, entry]

    def gathered(first, length):
        return jnp.concatenate(
            [
                jnp.concatenate([slots[row][first + j] for j in range(length)], axis=1)
                for row in range(rows)
            ],
            axis=0,
        )

    value = dense[...]
    turned = split(value.T)
    keep_outer_ref[...] = product(turned, split(gathered(rows + core * fetched, fetched)))
    send_outer_ref[...] = product(turned, split(gathered(rows + (1 - core) * fetched, fetched)))
    local = product(turned, split(gathered(0, rows)))
    whole[...] = product(split(local), split(value))
    keep_inner_ref[...] = whole[pl.ds(pl.multiple_of(core * half, half), half), :]
    send_inner_ref[:half, :] = whole[pl.ds(pl.multiple_of((1 - core) * half, half), half), :]


def window_kernel(held_ref, came_ref, *refs):
    ghosts, result_ref, prolong = refs[:-2], refs[-2], refs[-1]
    position = lax.axis_index("inner")
    core, chip = lax.rem(position, CORES), lax.div(position, CORES)
    chips = len(ghosts)
    size = ghosts[0].shape[0] // CORES
    for shift, ghost in enumerate(ghosts):
        for cross in range(CORES):
            source = lax.rem(chip + shift, chips) * CORES + lax.rem(core + cross, CORES)
            prolong[pl.ds(pl.multiple_of(source * size, size), size), :] = ghost[
                cross * size : (cross + 1) * size, :
            ]
    result_ref[...] = product(split(held_ref[...] + came_ref[...]), split(prolong[...]))


def store_blocks(value, blocks, out_hbm, first_row, first_column, sem):
    size = blocks.shape[-1]
    copies = []
    for g in range(value.shape[0] // size):
        for h in range(value.shape[1] // size):
            blocks[g, h] = value[g * size : (g + 1) * size, h * size : (h + 1) * size]
        copy = pltpu.make_async_copy(
            blocks.at[g],
            out_hbm.at[first_row + g, pl.ds(first_column, blocks.shape[1])],
            sem.at[g],
        )
        copy.start()
        copies.append(copy)
    return copies


def outer_kernel(other, value_ref, *refs):
    out_hbm, blocks, sem = refs[-3:]
    core = lax.rem(lax.axis_index("inner"), CORES)
    owner = 1 - core if other else core
    for copy in store_blocks(value_ref[...], blocks, out_hbm, 0, owner * 2 * CG, sem):
        copy.wait()


def inner_kernel(other, held_ref, came_ref, _, out_hbm, blocks, sem):
    core = lax.rem(lax.axis_index("inner"), CORES)
    owner = 1 - core if other else core
    first_row = owner * (CG // CORES)
    for copy in store_blocks(
        held_ref[...] + came_ref[...], blocks, out_hbm, first_row, CG, sem
    ):
        copy.wait()


VMEM = pl.BlockSpec(memory_space=pltpu.VMEM)
HBM = pl.BlockSpec(memory_space=pltpu.HBM)
PARAMS = pltpu.CompilerParams(vmem_limit_bytes=VMEM_BYTES)


def f32(*shape):
    return jax.ShapeDtypeStruct(shape, jnp.float32)


def per_device(
    operator_tiles,
    operator_cols,
    operator_count,
    prolong_tiles,
    prolong_cols,
    prolong_count,
    fetch_rows,
):
    rows, entries, size, _ = operator_tiles.shape
    subs, fetched = lax.axis_size("sub"), lax.axis_size("inner")
    chips = fetched // CORES
    width = CG * size
    half = width // CORES

    smem = pltpu.SMEM
    keep_outer, send_outer, keep_inner, send_inner, straight = pl.pallas_call(
        left_kernel,
        out_shape=[
            f32(width, fetched * size),
            f32(width, fetched * size),
            f32(half, width),
            f32(half + size, width),
            f32(size, width),
        ],
        in_specs=[HBM] * 7,
        out_specs=[VMEM] * 5,
        scratch_shapes=[
            smem(operator_cols.shape, jnp.int32),
            smem(operator_count.shape, jnp.int32),
            smem(prolong_cols.shape, jnp.int32),
            smem(prolong_count.shape, jnp.int32),
            smem((2,), jnp.int32),
            pltpu.VMEM(operator_tiles.shape, jnp.float32),
            pltpu.VMEM(prolong_tiles.shape, jnp.float32),
            pltpu.VMEM((rows * size, width), jnp.float32),
            pltpu.VMEM((width, width), jnp.float32),
        ]
        + [pltpu.VMEM((rows + 2 * fetched + 1, size, size), jnp.float32)] * rows
        + [pltpu.SemaphoreType.DMA((rows,)), pltpu.SemaphoreType.DMA((6,))],
        compiler_params=PARAMS,
        name="left",
    )(
        *(
            pltpu.with_memory_space_constraint(value, pltpu.HBM)
            for value in (
                operator_cols,
                operator_count,
                prolong_cols,
                prolong_count,
                fetch_rows.reshape(-1),
                operator_tiles,
                prolong_tiles,
            )
        )
    )

    swap_cores = [(i, i ^ 1) for i in range(fetched)]

    def other_core(value):
        return lax.ppermute(value, "inner", swap_cores)

    def chip_sum(value):
        step = 1
        while step < chips:
            came = lax.ppermute(
                value, "inner", [(i, i ^ (step * CORES)) for i in range(fetched)]
            )
            step *= 2
            if step < chips:
                value = value + came
        return value, came

    held_outer, came_outer = chip_sum(keep_outer + other_core(send_outer))
    arrived = other_core(send_inner)

    edge = jnp.concatenate([straight, arrived[half:]], axis=0)
    ghosts = []
    for shift in range(chips):
        pairs = []
        for sub in range(subs):
            for chip in range(chips):
                for core in range(CORES):
                    source_sub = sub - 1 if core == 0 else sub + 1
                    if 0 <= source_sub < subs:
                        source = (chip + shift) % chips * CORES + core
                        pairs.append(
                            (source_sub * fetched + source, sub * fetched + chip * CORES + core)
                        )
        ghosts.append(lax.ppermute(edge, ("sub", "inner"), pairs))

    held_inner, came_inner = chip_sum(keep_inner + arrived[:half])

    window = pl.pallas_call(
        window_kernel,
        out_shape=f32(width, width),
        in_specs=[VMEM] * (2 + len(ghosts)),
        out_specs=VMEM,
        scratch_shapes=[pltpu.VMEM((fetched * size, width), jnp.float32)],
        compiler_params=PARAMS,
        name="window",
    )(held_outer, came_outer, *ghosts)

    def store(kernel, rows, *values, out=None, name):
        outs = () if out is None else (out,)
        return pl.pallas_call(
            kernel,
            out_shape=f32(CG, 3 * CG, size, size),
            in_specs=[VMEM] * len(values) + [HBM] * len(outs),
            out_specs=HBM,
            scratch_shapes=[
                pltpu.VMEM((rows, CG, size, size), jnp.float32),
                pltpu.SemaphoreType.DMA((rows,)),
            ],
            input_output_aliases={len(values): 0} if outs else {},
            compiler_params=PARAMS,
            name=name,
        )(*values, *outs)

    own = functools.partial
    out = store(own(outer_kernel, False), CG, window, name="outer_own")
    out = store(own(outer_kernel, True), CG, other_core(window), out=out, name="outer_other")
    out = store(
        own(inner_kernel, False), CG // CORES, held_inner, came_inner, out=out, name="inner_own"
    )
    return store(
        own(inner_kernel, True),
        CG // CORES,
        other_core(held_inner),
        other_core(came_inner),
        out=out,
        name="inner_other",
    )


def solution(mesh):
    placed = (
        P(("sub", "inner"), None, None, None),
        P(("sub", "inner"), None),
        P(("sub", "inner")),
        P(("sub", "inner"), None, None, None),
        P(("sub", "inner"), None),
        P(("sub", "inner")),
        P(("sub", "inner"), None),
    )
    return jax.shard_map(
        per_device,
        mesh=mesh,
        in_specs=placed,
        out_specs=P("sub", None, None, None),
        check_vma=False,
    )
```

```python
import functools

import jax
import jax.numpy as jnp
from jax import lax
from jax.experimental import pallas as pl
from jax.experimental.pallas import tpu as pltpu
from jax.sharding import PartitionSpec as P

CG = 4
CORES = 2
VMEM_BYTES = 32 * 1024 * 1024


def split(value):
    high = value.astype(jnp.bfloat16)
    low = (value - high.astype(jnp.float32)).astype(jnp.bfloat16)
    return high, low


def product(left, right):
    dot = functools.partial(jnp.dot, preferred_element_type=jnp.float32)
    return dot(left[0], right[0]) + (dot(left[1], right[0]) + dot(left[0], right[1]))


def left_kernel(
    cols_hbm,
    count_hbm,
    prolong_cols_hbm,
    prolong_count_hbm,
    fetch_hbm,
    tiles_hbm,
    prolong_hbm,
    keep_outer_ref,
    send_outer_ref,
    keep_inner_ref,
    send_inner_ref,
    straight_ref,
    cols,
    count,
    prolong_cols,
    prolong_count,
    fetch,
    tiles,
    prolong,
    dense,
    whole,
    *rest,
):
    slots, (tile_sems, small_sems) = rest[:-2], rest[-2:]
    rows, entries, size, _ = tiles.shape
    fetched = keep_outer_ref.shape[1] // size
    smalls = [
        pltpu.make_async_copy(source, target, small_sems.at[index])
        for index, (source, target) in enumerate(
            (
                (prolong_cols_hbm, prolong_cols),
                (prolong_count_hbm, prolong_count),
                (fetch_hbm, fetch),
                (cols_hbm, cols),
                (count_hbm, count),
                (prolong_hbm, prolong),
            )
        )
    ]
    copies = [
        pltpu.make_async_copy(tiles_hbm.at[row], tiles.at[row], tile_sems.at[row])
        for row in range(rows)
    ]
    for copy in smalls + copies:
        copy.start()
    for ref in slots:
        ref[...] = jnp.zeros_like(ref)
    first_coarse = lax.axis_index("sub") * CG
    core = lax.rem(lax.axis_index("inner"), CORES)
    for copy in smalls:
        copy.wait()

    for row in range(rows):
        blocks = []
        for coarse in range(CG):
            block = None
            for m in range(prolong.shape[1]):
                hit = (prolong_cols[row, m] == first_coarse + coarse) & (m < prolong_count[row])
                term = prolong[row, m] * jnp.where(hit, 1.0, 0.0)
                block = term if block is None else block + term
            blocks.append(block)
        dense[row * size : (row + 1) * size, :] = jnp.concatenate(blocks, axis=1)

    half = keep_inner_ref.shape[0]
    straight_ref[...] = dense[pl.ds(pl.multiple_of(fetch[core] * size, size), size), :]
    send_inner_ref[half:, :] = dense[pl.ds(pl.multiple_of(fetch[1 - core] * size, size), size), :]

    for first in range(0, rows, 2):
        pair = range(first, min(first + 2, rows))
        for row in pair:
            copies[row].wait()
        for entry in range(entries):
            for row in pair:
                slot = jnp.where(entry < count[row], cols[row, entry], rows + 2 * fetched)
                slots[row][slot] += tiles[row, entry]

    def gathered(first, length):
        return jnp.concatenate(
            [
                jnp.concatenate([slots[row][first + j] for j in range(length)], axis=1)
                for row in range(rows)
            ],
            axis=0,
        )

    value = dense[...]
    turned = split(value.T)
    keep_outer_ref[...] = product(turned, split(gathered(rows + core * fetched, fetched)))
    send_outer_ref[...] = product(turned, split(gathered(rows + (1 - core) * fetched, fetched)))
    local = product(turned, split(gathered(0, rows)))
    whole[...] = product(split(local), split(value))
    keep_inner_ref[...] = whole[pl.ds(pl.multiple_of(core * half, half), half), :]
    send_inner_ref[:half, :] = whole[pl.ds(pl.multiple_of((1 - core) * half, half), half), :]


def window_kernel(held_ref, came_ref, *refs):
    ghosts, result_ref, prolong = refs[:-2], refs[-2], refs[-1]
    position = lax.axis_index("inner")
    core, chip = lax.rem(position, CORES), lax.div(position, CORES)
    chips = len(ghosts)
    size = ghosts[0].shape[0] // CORES
    for shift, ghost in enumerate(ghosts):
        for cross in range(CORES):
            source = lax.rem(shift - chip + chips, chips) * CORES + lax.rem(1 - core + cross, CORES)
            prolong[pl.ds(pl.multiple_of(source * size, size), size), :] = ghost[
                cross * size : (cross + 1) * size, :
            ]
    result_ref[...] = product(split(held_ref[...] + came_ref[...]), split(prolong[...]))


def store_kernel(other, window_ref, held_ref, came_ref, *refs):
    out_hbm, outer, inner, outer_sem, inner_sem = refs[-5:]
    core = lax.rem(lax.axis_index("inner"), CORES)
    owner = 1 - core if other else core
    size = outer.shape[-1]
    copies = []

    def store(value, blocks, first_row, first_column, sem):
        for g in range(blocks.shape[0]):
            for h in range(blocks.shape[1]):
                blocks[g, h] = value[g * size : (g + 1) * size, h * size : (h + 1) * size]
            copy = pltpu.make_async_copy(
                blocks.at[g],
                out_hbm.at[first_row + g, pl.ds(first_column, blocks.shape[1])],
                sem.at[g],
            )
            copy.start()
            copies.append(copy)

    store(window_ref[...], outer, 0, owner * 2 * CG, outer_sem)
    store(held_ref[...] + came_ref[...], inner, owner * (CG // CORES), CG, inner_sem)
    for copy in copies:
        copy.wait()


VMEM = pl.BlockSpec(memory_space=pltpu.VMEM)
HBM = pl.BlockSpec(memory_space=pltpu.HBM)
PARAMS = pltpu.CompilerParams(vmem_limit_bytes=VMEM_BYTES)


def f32(*shape):
    return jax.ShapeDtypeStruct(shape, jnp.float32)


def per_device(
    operator_tiles,
    operator_cols,
    operator_count,
    prolong_tiles,
    prolong_cols,
    prolong_count,
    fetch_rows,
):
    rows, entries, size, _ = operator_tiles.shape
    subs, fetched = lax.axis_size("sub"), lax.axis_size("inner")
    chips = fetched // CORES
    width = CG * size
    half = width // CORES

    smem = pltpu.SMEM
    keep_outer, send_outer, keep_inner, send_inner, straight = pl.pallas_call(
        left_kernel,
        out_shape=[
            f32(width, fetched * size),
            f32(width, fetched * size),
            f32(half, width),
            f32(half + size, width),
            f32(size, width),
        ],
        in_specs=[HBM] * 7,
        out_specs=[VMEM] * 5,
        scratch_shapes=[
            smem(operator_cols.shape, jnp.int32),
            smem(operator_count.shape, jnp.int32),
            smem(prolong_cols.shape, jnp.int32),
            smem(prolong_count.shape, jnp.int32),
            smem((2,), jnp.int32),
            pltpu.VMEM(operator_tiles.shape, jnp.float32),
            pltpu.VMEM(prolong_tiles.shape, jnp.float32),
            pltpu.VMEM((rows * size, width), jnp.float32),
            pltpu.VMEM((width, width), jnp.float32),
        ]
        + [pltpu.VMEM((rows + 2 * fetched + 1, size, size), jnp.float32)] * rows
        + [pltpu.SemaphoreType.DMA((rows,)), pltpu.SemaphoreType.DMA((6,))],
        compiler_params=PARAMS,
        name="left",
    )(
        *(
            pltpu.with_memory_space_constraint(value, pltpu.HBM)
            for value in (
                operator_cols,
                operator_count,
                prolong_cols,
                prolong_count,
                fetch_rows.reshape(-1),
                operator_tiles,
                prolong_tiles,
            )
        )
    )

    swap_cores = [(i, i ^ 1) for i in range(fetched)]

    def other_core(value):
        return lax.ppermute(value, "inner", swap_cores)

    def chip_sum(value):
        step = 1
        while step < chips:
            came = lax.ppermute(
                value, "inner", [(i, i ^ (step * CORES)) for i in range(fetched)]
            )
            step *= 2
            if step < chips:
                value = value + came
        return value, came

    held_outer, came_outer = chip_sum(keep_outer + other_core(send_outer))
    arrived = other_core(send_inner)

    edge = jnp.concatenate([straight, arrived[half:]], axis=0)
    ghosts = []
    for shift in range(chips):
        pairs = []
        for sub in range(subs - 1):
            for chip in range(chips):
                below = (sub * chips + chip) * CORES + 1
                above = ((sub + 1) * chips + (shift - chip) % chips) * CORES
                pairs += [(below, above), (above, below)]
        ghosts.append(lax.ppermute(edge, ("sub", "inner"), pairs))

    held_inner, came_inner = chip_sum(keep_inner + arrived[:half])

    window = pl.pallas_call(
        window_kernel,
        out_shape=f32(width, width),
        in_specs=[VMEM] * (2 + len(ghosts)),
        out_specs=VMEM,
        scratch_shapes=[pltpu.VMEM((fetched * size, width), jnp.float32)],
        compiler_params=PARAMS,
        name="window",
    )(held_outer, came_outer, *ghosts)

    def store(other, *values):
        return pl.pallas_call(
            functools.partial(store_kernel, other),
            out_shape=f32(CG, 3 * CG, size, size),
            in_specs=[VMEM] * 3 + [HBM] * (len(values) - 3),
            out_specs=HBM,
            scratch_shapes=[
                pltpu.VMEM((CG, CG, size, size), jnp.float32),
                pltpu.VMEM((CG // CORES, CG, size, size), jnp.float32),
                pltpu.SemaphoreType.DMA((CG,)),
                pltpu.SemaphoreType.DMA((CG // CORES,)),
            ],
            input_output_aliases={3: 0} if other else {},
            compiler_params=PARAMS,
            name="store_other" if other else "store_own",
        )(*values)

    own = (window, held_inner, came_inner)
    return store(True, *map(other_core, own), store(False, *own))


def solution(mesh):
    placed = (
        P(("sub", "inner"), None, None, None),
        P(("sub", "inner"), None),
        P(("sub", "inner")),
        P(("sub", "inner"), None, None, None),
        P(("sub", "inner"), None),
        P(("sub", "inner")),
        P(("sub", "inner"), None),
    )
    return jax.shard_map(
        per_device,
        mesh=mesh,
        in_specs=placed,
        out_specs=P("sub", None, None, None),
        check_vma=False,
    )
```

```python
import functools

import jax
import jax.numpy as jnp
from jax import lax
from jax.experimental import pallas as pl
from jax.experimental.pallas import tpu as pltpu
from jax.sharding import PartitionSpec as P

CG = 4
CORES = 2
META = 8
VMEM_BYTES = 32 * 1024 * 1024


def split(value):
    high = value.astype(jnp.bfloat16)
    low = (value - high.astype(jnp.float32)).astype(jnp.bfloat16)
    return high, low


def product(left, right):
    dot = functools.partial(jnp.dot, preferred_element_type=jnp.float32)
    return dot(left[0], right[0]) + (dot(left[1], right[0]) + dot(left[0], right[1]))


def left_kernel(
    cols_hbm,
    count_hbm,
    prolong_cols_hbm,
    prolong_count_hbm,
    fetch_hbm,
    tiles_hbm,
    prolong_hbm,
    keep_outer_ref,
    send_outer_ref,
    keep_inner_ref,
    send_inner_ref,
    straight_ref,
    cols,
    count,
    prolong_cols,
    prolong_count,
    fetch,
    tiles,
    prolong,
    dense,
    whole,
    *rest,
):
    slots, (tile_sems, small_sems) = rest[:-2], rest[-2:]
    rows, entries, size, _ = tiles.shape
    fetched = keep_outer_ref.shape[1] // size
    smalls = [
        pltpu.make_async_copy(source, target, small_sems.at[index])
        for index, (source, target) in enumerate(
            (
                (prolong_cols_hbm, prolong_cols),
                (prolong_count_hbm, prolong_count),
                (fetch_hbm, fetch),
                (cols_hbm, cols),
                (count_hbm, count),
                (prolong_hbm, prolong),
            )
        )
    ]
    copies = [
        pltpu.make_async_copy(tiles_hbm.at[row], tiles.at[row], tile_sems.at[row])
        for row in range(rows)
    ]
    for copy in smalls + copies:
        copy.start()
    for ref in slots:
        ref[...] = jnp.zeros_like(ref)
    first_coarse = lax.axis_index("sub") * CG
    core = lax.rem(lax.axis_index("inner"), CORES)
    for copy in smalls:
        copy.wait()

    for row in range(rows):
        blocks = []
        for coarse in range(CG):
            block = None
            for m in range(prolong.shape[1]):
                hit = (prolong_cols[row, m] == first_coarse + coarse) & (m < prolong_count[row])
                term = prolong[row, m] * jnp.where(hit, 1.0, 0.0)
                block = term if block is None else block + term
            blocks.append(block)
        dense[row * size : (row + 1) * size, :] = jnp.concatenate(blocks, axis=1)

    half = keep_inner_ref.shape[0]
    packed = straight_ref.shape[0] - META
    quarter = size // CG
    line = lax.broadcasted_iota(jnp.int32, (META, CG * size), 0)
    lane = lax.broadcasted_iota(jnp.int32, (META, CG * size), 1)
    for cross, (ref, first) in enumerate(((straight_ref, 0), (send_inner_ref, half))):
        row = fetch[core if cross == 0 else 1 - core]
        meta = jnp.zeros((META, CG * size), jnp.float32)
        for m in range(prolong.shape[1]):
            tile = prolong[row, m]
            ref[first + m * quarter : first + (m + 1) * quarter, :] = jnp.concatenate(
                [tile[part * quarter : (part + 1) * quarter, :] for part in range(CG)], axis=1
            )
            column = jnp.where(
                m < prolong_count[row], prolong_cols[row, m] - first_coarse, -1
            ).astype(jnp.float32)
            meta = jnp.where((line == cross) & (lane == m), column, meta)
        ref[first + packed : first + packed + META, :] = meta

    for first in range(0, rows, 2):
        pair = range(first, min(first + 2, rows))
        for row in pair:
            copies[row].wait()
        for entry in range(entries):
            for row in pair:
                slot = jnp.where(entry < count[row], cols[row, entry], rows + 2 * fetched)
                slots[row][slot] += tiles[row, entry]

    def gathered(first, length):
        return jnp.concatenate(
            [
                jnp.concatenate([slots[row][first + j] for j in range(length)], axis=1)
                for row in range(rows)
            ],
            axis=0,
        )

    value = dense[...]
    turned = split(value.T)
    keep_outer_ref[...] = product(turned, split(gathered(rows + core * fetched, fetched)))
    send_outer_ref[...] = product(turned, split(gathered(rows + (1 - core) * fetched, fetched)))
    local = product(turned, split(gathered(0, rows)))
    whole[...] = product(split(local), split(value))
    keep_inner_ref[...] = whole[pl.ds(pl.multiple_of(core * half, half), half), :]
    send_inner_ref[:half, :] = whole[pl.ds(pl.multiple_of((1 - core) * half, half), half), :]


def window_kernel(held_ref, came_ref, *refs):
    ghosts, result_ref, prolong = refs[:-2], refs[-2], refs[-1]
    position = lax.axis_index("inner")
    core, chip = lax.rem(position, CORES), lax.div(position, CORES)
    chips = len(ghosts)
    size = result_ref.shape[0] // CG
    quarter = size // CG
    packed = (ghosts[0].shape[0] - META) // CORES
    for shift, ghost in enumerate(ghosts):
        for cross in range(CORES):
            source = lax.rem(shift - chip + chips, chips) * CORES + lax.rem(1 - core + cross, CORES)
            blocks = [None] * CG
            for m in range(packed // quarter):
                first = cross * packed + m * quarter
                column = ghost[CORES * packed + cross : CORES * packed + cross + 1, m : m + 1]
                tile = jnp.concatenate(
                    [
                        ghost[first : first + quarter, part * size : (part + 1) * size]
                        for part in range(CG)
                    ],
                    axis=0,
                )
                for coarse in range(CG):
                    term = tile * jnp.where(column == coarse, 1.0, 0.0)
                    blocks[coarse] = term if m == 0 else blocks[coarse] + term
            prolong[pl.ds(pl.multiple_of(source * size, size), size), :] = jnp.concatenate(
                blocks, axis=1
            )
    result_ref[...] = product(split(held_ref[...] + came_ref[...]), split(prolong[...]))


def store_kernel(other, window_ref, held_ref, came_ref, *refs):
    out_hbm, outer, inner, outer_sem, inner_sem = refs[-5:]
    core = lax.rem(lax.axis_index("inner"), CORES)
    owner = 1 - core if other else core
    size = outer.shape[-1]
    copies = []

    def store(value, blocks, first_row, first_column, sem):
        for g in range(blocks.shape[0]):
            for h in range(blocks.shape[1]):
                blocks[g, h] = value[g * size : (g + 1) * size, h * size : (h + 1) * size]
            copy = pltpu.make_async_copy(
                blocks.at[g],
                out_hbm.at[first_row + g, pl.ds(first_column, blocks.shape[1])],
                sem.at[g],
            )
            copy.start()
            copies.append(copy)

    store(window_ref[...], outer, 0, owner * 2 * CG, outer_sem)
    store(held_ref[...] + came_ref[...], inner, owner * (CG // CORES), CG, inner_sem)
    for copy in copies:
        copy.wait()


VMEM = pl.BlockSpec(memory_space=pltpu.VMEM)
HBM = pl.BlockSpec(memory_space=pltpu.HBM)
PARAMS = pltpu.CompilerParams(vmem_limit_bytes=VMEM_BYTES)


def f32(*shape):
    return jax.ShapeDtypeStruct(shape, jnp.float32)


def per_device(
    operator_tiles,
    operator_cols,
    operator_count,
    prolong_tiles,
    prolong_cols,
    prolong_count,
    fetch_rows,
):
    rows, entries, size, _ = operator_tiles.shape
    subs, fetched = lax.axis_size("sub"), lax.axis_size("inner")
    chips = fetched // CORES
    width = CG * size
    half = width // CORES
    packed = prolong_tiles.shape[1] * size // CG

    smem = pltpu.SMEM
    keep_outer, send_outer, keep_inner, send_inner, straight = pl.pallas_call(
        left_kernel,
        out_shape=[
            f32(width, fetched * size),
            f32(width, fetched * size),
            f32(half, width),
            f32(half + packed + META, width),
            f32(packed + META, width),
        ],
        in_specs=[HBM] * 7,
        out_specs=[VMEM] * 5,
        scratch_shapes=[
            smem(operator_cols.shape, jnp.int32),
            smem(operator_count.shape, jnp.int32),
            smem(prolong_cols.shape, jnp.int32),
            smem(prolong_count.shape, jnp.int32),
            smem((2,), jnp.int32),
            pltpu.VMEM(operator_tiles.shape, jnp.float32),
            pltpu.VMEM(prolong_tiles.shape, jnp.float32),
            pltpu.VMEM((rows * size, width), jnp.float32),
            pltpu.VMEM((width, width), jnp.float32),
        ]
        + [pltpu.VMEM((rows + 2 * fetched + 1, size, size), jnp.float32)] * rows
        + [pltpu.SemaphoreType.DMA((rows,)), pltpu.SemaphoreType.DMA((6,))],
        compiler_params=PARAMS,
        name="left",
    )(
        *(
            pltpu.with_memory_space_constraint(value, pltpu.HBM)
            for value in (
                operator_cols,
                operator_count,
                prolong_cols,
                prolong_count,
                fetch_rows.reshape(-1),
                operator_tiles,
                prolong_tiles,
            )
        )
    )

    swap_cores = [(i, i ^ 1) for i in range(fetched)]

    def other_core(value):
        return lax.ppermute(value, "inner", swap_cores)

    def chip_sum(value):
        step = 1
        while step < chips:
            came = lax.ppermute(
                value, "inner", [(i, i ^ (step * CORES)) for i in range(fetched)]
            )
            step *= 2
            if step < chips:
                value = value + came
        return value, came

    held_outer, came_outer = chip_sum(keep_outer + other_core(send_outer))
    arrived = other_core(send_inner)

    crossed = arrived[half:]
    edge = jnp.concatenate(
        [straight[:packed], crossed[:packed], straight[packed:] + crossed[packed:]], axis=0
    )
    ghosts = []
    for shift in range(chips):
        pairs = []
        for sub in range(subs - 1):
            for chip in range(chips):
                below = (sub * chips + chip) * CORES + 1
                above = ((sub + 1) * chips + (shift - chip) % chips) * CORES
                pairs += [(below, above), (above, below)]
        ghosts.append(lax.ppermute(edge, ("sub", "inner"), pairs))

    held_inner, came_inner = chip_sum(keep_inner + arrived[:half])

    window = pl.pallas_call(
        window_kernel,
        out_shape=f32(width, width),
        in_specs=[VMEM] * (2 + len(ghosts)),
        out_specs=VMEM,
        scratch_shapes=[pltpu.VMEM((fetched * size, width), jnp.float32)],
        compiler_params=PARAMS,
        name="window",
    )(held_outer, came_outer, *ghosts)

    def store(other, *values):
        return pl.pallas_call(
            functools.partial(store_kernel, other),
            out_shape=f32(CG, 3 * CG, size, size),
            in_specs=[VMEM] * 3 + [HBM] * (len(values) - 3),
            out_specs=HBM,
            scratch_shapes=[
                pltpu.VMEM((CG, CG, size, size), jnp.float32),
                pltpu.VMEM((CG // CORES, CG, size, size), jnp.float32),
                pltpu.SemaphoreType.DMA((CG,)),
                pltpu.SemaphoreType.DMA((CG // CORES,)),
            ],
            input_output_aliases={3: 0} if other else {},
            compiler_params=PARAMS,
            name="store_other" if other else "store_own",
        )(*values)

    own = (window, held_inner, came_inner)
    return store(True, *map(other_core, own), store(False, *own))


def solution(mesh):
    placed = (
        P(("sub", "inner"), None, None, None),
        P(("sub", "inner"), None),
        P(("sub", "inner")),
        P(("sub", "inner"), None, None, None),
        P(("sub", "inner"), None),
        P(("sub", "inner")),
        P(("sub", "inner"), None),
    )
    return jax.shard_map(
        per_device,
        mesh=mesh,
        in_specs=placed,
        out_specs=P("sub", None, None, None),
        check_vma=False,
    )
```

```python
import functools

import jax
import jax.numpy as jnp
from jax import lax
from jax.experimental import pallas as pl
from jax.experimental.pallas import tpu as pltpu
from jax.sharding import PartitionSpec as P

CG = 4
CORES = 2
META = 8
VMEM_BYTES = 32 * 1024 * 1024


def split(value):
    high = value.astype(jnp.bfloat16)
    low = (value - high.astype(jnp.float32)).astype(jnp.bfloat16)
    return high, low


def product(left, right):
    dot = functools.partial(jnp.dot, preferred_element_type=jnp.float32)
    return dot(left[0], right[0]) + (dot(left[1], right[0]) + dot(left[0], right[1]))


def left_kernel(
    cols_hbm,
    count_hbm,
    prolong_cols_hbm,
    prolong_count_hbm,
    fetch_hbm,
    tiles_hbm,
    prolong_hbm,
    send_outer_ref,
    outer_ref,
    local_ref,
    dense,
    straight_ref,
    crossed_ref,
    cols,
    count,
    prolong_cols,
    prolong_count,
    fetch,
    tiles,
    prolong,
    *rest,
):
    slots, (tile_sems, small_sems) = rest[:-2], rest[-2:]
    rows, entries, size, _ = tiles.shape
    fetched = outer_ref.shape[1] // size
    smalls = [
        pltpu.make_async_copy(source, target, small_sems.at[index])
        for index, (source, target) in enumerate(
            (
                (prolong_cols_hbm, prolong_cols),
                (prolong_count_hbm, prolong_count),
                (fetch_hbm, fetch),
                (cols_hbm, cols),
                (count_hbm, count),
                (prolong_hbm, prolong),
            )
        )
    ]
    copies = [
        pltpu.make_async_copy(tiles_hbm.at[row], tiles.at[row], tile_sems.at[row])
        for row in range(rows)
    ]
    for copy in smalls + copies:
        copy.start()
    for ref in slots:
        ref[...] = jnp.zeros_like(ref)
    first_coarse = lax.axis_index("sub") * CG
    core = lax.rem(lax.axis_index("inner"), CORES)
    for copy in smalls:
        copy.wait()

    for row in range(rows):
        blocks = []
        for coarse in range(CG):
            block = None
            for m in range(prolong.shape[1]):
                hit = (prolong_cols[row, m] == first_coarse + coarse) & (m < prolong_count[row])
                term = prolong[row, m] * jnp.where(hit, 1.0, 0.0)
                block = term if block is None else block + term
            blocks.append(block)
        dense[row * size : (row + 1) * size, :] = jnp.concatenate(blocks, axis=1)

    packed = straight_ref.shape[0] - META
    quarter = size // CG
    line = lax.broadcasted_iota(jnp.int32, (META, CG * size), 0)
    lane = lax.broadcasted_iota(jnp.int32, (META, CG * size), 1)
    for cross, ref in enumerate((straight_ref, crossed_ref)):
        row = fetch[core if cross == 0 else 1 - core]
        meta = jnp.zeros((META, CG * size), jnp.float32)
        for m in range(prolong.shape[1]):
            tile = prolong[row, m]
            ref[m * quarter : (m + 1) * quarter, :] = jnp.concatenate(
                [tile[part * quarter : (part + 1) * quarter, :] for part in range(CG)], axis=1
            )
            column = jnp.where(
                m < prolong_count[row], prolong_cols[row, m] - first_coarse, -1
            ).astype(jnp.float32)
            meta = jnp.where((line == cross) & (lane == m), column, meta)
        ref[packed:, :] = meta

    for first in range(0, rows, 2):
        pair = range(first, min(first + 2, rows))
        for row in pair:
            copies[row].wait()
        for entry in range(entries):
            for row in pair:
                slot = jnp.where(entry < count[row], cols[row, entry], rows + 2 * fetched)
                slots[row][slot] += tiles[row, entry]

    def gathered(first, length):
        return jnp.concatenate(
            [
                jnp.concatenate([slots[row][first + j] for j in range(length)], axis=1)
                for row in range(rows)
            ],
            axis=0,
        )

    turned = split(dense[...].T)
    send_outer_ref[...] = product(turned, split(gathered(rows + (1 - core) * fetched, fetched)))
    outer_ref[...] = gathered(rows + core * fetched, fetched)
    local_ref[...] = gathered(0, rows)


def middle_kernel(dense_ref, outer_ref, local_ref, outer_keep_ref, keep_ref, send_ref, whole):
    core = lax.rem(lax.axis_index("inner"), CORES)
    half = keep_ref.shape[0]
    value = dense_ref[...]
    turned = split(value.T)
    outer_keep_ref[...] = product(turned, split(outer_ref[...]))
    applied = product(split(local_ref[...]), split(value))
    whole[...] = product(turned, split(applied))
    for ref, side in ((keep_ref, core), (send_ref, 1 - core)):
        ref[...] = whole[pl.ds(pl.multiple_of(side * half, half), half), :]


def window_kernel(held_ref, came_ref, *refs):
    ghosts, result_ref, prolong = refs[:-2], refs[-2], refs[-1]
    position = lax.axis_index("inner")
    core, chip = lax.rem(position, CORES), lax.div(position, CORES)
    chips = len(ghosts)
    size = result_ref.shape[0] // CG
    quarter = size // CG
    packed = (ghosts[0].shape[0] - META) // CORES
    for shift, ghost in enumerate(ghosts):
        for cross in range(CORES):
            source = lax.rem(shift - chip + chips, chips) * CORES + lax.rem(1 - core + cross, CORES)
            blocks = [None] * CG
            for m in range(packed // quarter):
                first = cross * packed + m * quarter
                column = ghost[CORES * packed + cross : CORES * packed + cross + 1, m : m + 1]
                tile = jnp.concatenate(
                    [
                        ghost[first : first + quarter, part * size : (part + 1) * size]
                        for part in range(CG)
                    ],
                    axis=0,
                )
                for coarse in range(CG):
                    term = tile * jnp.where(column == coarse, 1.0, 0.0)
                    blocks[coarse] = term if m == 0 else blocks[coarse] + term
            prolong[pl.ds(pl.multiple_of(source * size, size), size), :] = jnp.concatenate(
                blocks, axis=1
            )
    result_ref[...] = product(split(held_ref[...] + came_ref[...]), split(prolong[...]))


def store_kernel(other, window_ref, middle_ref, *refs):
    out_hbm, outer, inner, outer_sem, inner_sem = refs[-5:]
    core = lax.rem(lax.axis_index("inner"), CORES)
    owner = 1 - core if other else core
    size = outer.shape[-1]
    copies = []

    def store(value, blocks, first_row, first_column, sem):
        for g in range(blocks.shape[0]):
            for h in range(blocks.shape[1]):
                blocks[g, h] = value[g * size : (g + 1) * size, h * size : (h + 1) * size]
            copy = pltpu.make_async_copy(
                blocks.at[g],
                out_hbm.at[first_row + g, pl.ds(first_column, blocks.shape[1])],
                sem.at[g],
            )
            copy.start()
            copies.append(copy)

    store(window_ref[...], outer, 0, owner * 2 * CG, outer_sem)
    store(middle_ref[...], inner, owner * (CG // CORES), CG, inner_sem)
    for copy in copies:
        copy.wait()


VMEM = pl.BlockSpec(memory_space=pltpu.VMEM)
HBM = pl.BlockSpec(memory_space=pltpu.HBM)
PARAMS = pltpu.CompilerParams(vmem_limit_bytes=VMEM_BYTES)


def f32(*shape):
    return jax.ShapeDtypeStruct(shape, jnp.float32)


def per_device(
    operator_tiles,
    operator_cols,
    operator_count,
    prolong_tiles,
    prolong_cols,
    prolong_count,
    fetch_rows,
):
    rows, entries, size, _ = operator_tiles.shape
    subs, fetched = lax.axis_size("sub"), lax.axis_size("inner")
    chips = fetched // CORES
    width = CG * size
    half = width // CORES
    packed = prolong_tiles.shape[1] * size // CG

    smem = pltpu.SMEM
    send_outer, outer, local, dense, straight, crossed = pl.pallas_call(
        left_kernel,
        out_shape=[
            f32(width, fetched * size),
            f32(rows * size, fetched * size),
            f32(rows * size, rows * size),
            f32(rows * size, width),
            f32(packed + META, width),
            f32(packed + META, width),
        ],
        in_specs=[HBM] * 7,
        out_specs=[VMEM] * 6,
        scratch_shapes=[
            smem(operator_cols.shape, jnp.int32),
            smem(operator_count.shape, jnp.int32),
            smem(prolong_cols.shape, jnp.int32),
            smem(prolong_count.shape, jnp.int32),
            smem((2,), jnp.int32),
            pltpu.VMEM(operator_tiles.shape, jnp.float32),
            pltpu.VMEM(prolong_tiles.shape, jnp.float32),
        ]
        + [pltpu.VMEM((rows + 2 * fetched + 1, size, size), jnp.float32)] * rows
        + [pltpu.SemaphoreType.DMA((rows,)), pltpu.SemaphoreType.DMA((6,))],
        compiler_params=PARAMS,
        name="left",
    )(
        *(
            pltpu.with_memory_space_constraint(value, pltpu.HBM)
            for value in (
                operator_cols,
                operator_count,
                prolong_cols,
                prolong_count,
                fetch_rows.reshape(-1),
                operator_tiles,
                prolong_tiles,
            )
        )
    )

    keep_outer, keep_inner, send_inner = pl.pallas_call(
        middle_kernel,
        out_shape=[f32(width, fetched * size), f32(half, width), f32(half, width)],
        in_specs=[VMEM] * 3,
        out_specs=[VMEM] * 3,
        scratch_shapes=[pltpu.VMEM((width, width), jnp.float32)],
        compiler_params=PARAMS,
        name="middle",
    )(dense, outer, local)

    swap_cores = [(i, i ^ 1) for i in range(fetched)]

    def other_core(value):
        return lax.ppermute(value, "inner", swap_cores)

    def chip_sum(value):
        step = 1
        while step < chips:
            came = lax.ppermute(
                value, "inner", [(i, i ^ (step * CORES)) for i in range(fetched)]
            )
            step *= 2
            if step < chips:
                value = value + came
        return value, came

    held_outer, came_outer = chip_sum(keep_outer + other_core(send_outer))
    crossed = other_core(crossed)
    edge = jnp.concatenate(
        [straight[:packed], crossed[:packed], straight[packed:] + crossed[packed:]], axis=0
    )
    ghosts = []
    for shift in range(chips):
        pairs = []
        for sub in range(subs - 1):
            for chip in range(chips):
                below = (sub * chips + chip) * CORES + 1
                above = ((sub + 1) * chips + (shift - chip) % chips) * CORES
                pairs += [(below, above), (above, below)]
        ghosts.append(lax.ppermute(edge, ("sub", "inner"), pairs))

    held_inner, came_inner = chip_sum(keep_inner + other_core(send_inner))

    window = pl.pallas_call(
        window_kernel,
        out_shape=f32(width, width),
        in_specs=[VMEM] * (2 + len(ghosts)),
        out_specs=VMEM,
        scratch_shapes=[pltpu.VMEM((fetched * size, width), jnp.float32)],
        compiler_params=PARAMS,
        name="window",
    )(held_outer, came_outer, *ghosts)

    def store(other, *values):
        return pl.pallas_call(
            functools.partial(store_kernel, other),
            out_shape=f32(CG, 3 * CG, size, size),
            in_specs=[VMEM] * 2 + [HBM] * (len(values) - 2),
            out_specs=HBM,
            scratch_shapes=[
                pltpu.VMEM((CG, CG, size, size), jnp.float32),
                pltpu.VMEM((CG // CORES, CG, size, size), jnp.float32),
                pltpu.SemaphoreType.DMA((CG,)),
                pltpu.SemaphoreType.DMA((CG // CORES,)),
            ],
            input_output_aliases={2: 0} if other else {},
            compiler_params=PARAMS,
            name="store_other" if other else "store_own",
        )(*values)

    own = (window, held_inner + came_inner)
    return store(True, *map(other_core, own), store(False, *own))


def solution(mesh):
    placed = (
        P(("sub", "inner"), None, None, None),
        P(("sub", "inner"), None),
        P(("sub", "inner")),
        P(("sub", "inner"), None, None, None),
        P(("sub", "inner"), None),
        P(("sub", "inner")),
        P(("sub", "inner"), None),
    )
    return jax.shard_map(
        per_device,
        mesh=mesh,
        in_specs=placed,
        out_specs=P("sub", None, None, None),
        check_vma=False,
    )
```

```python
import functools

import jax
import jax.numpy as jnp
from jax import lax
from jax.experimental import pallas as pl
from jax.experimental.pallas import tpu as pltpu
from jax.sharding import PartitionSpec as P

CG = 4
CORES = 2
META = 8
VMEM_BYTES = 32 * 1024 * 1024


def split(value):
    high = value.astype(jnp.bfloat16)
    low = (value - high.astype(jnp.float32)).astype(jnp.bfloat16)
    return high, low


def product(left, right):
    dot = functools.partial(jnp.dot, preferred_element_type=jnp.float32)
    return dot(left[0], right[0]) + (dot(left[1], right[0]) + dot(left[0], right[1]))


def left_kernel(
    cols_hbm,
    count_hbm,
    prolong_cols_hbm,
    prolong_count_hbm,
    fetch_hbm,
    tiles_hbm,
    prolong_hbm,
    send_outer_ref,
    outer_ref,
    local_ref,
    dense,
    straight_ref,
    crossed_ref,
    cols,
    count,
    prolong_cols,
    prolong_count,
    fetch,
    tiles,
    prolong,
    *rest,
):
    slots, (tile_sems, small_sems) = rest[:-2], rest[-2:]
    rows, entries, size, _ = tiles.shape
    fetched = outer_ref.shape[1] // size
    smalls = [
        pltpu.make_async_copy(source, target, small_sems.at[index])
        for index, (source, target) in enumerate(
            (
                (prolong_cols_hbm, prolong_cols),
                (prolong_count_hbm, prolong_count),
                (fetch_hbm, fetch),
                (cols_hbm, cols),
                (count_hbm, count),
                (prolong_hbm, prolong),
            )
        )
    ]
    copies = [
        pltpu.make_async_copy(tiles_hbm.at[row], tiles.at[row], tile_sems.at[row])
        for row in range(rows)
    ]
    for copy in smalls + copies:
        copy.start()
    for ref in slots:
        ref[...] = jnp.zeros_like(ref)
    first_coarse = lax.axis_index("sub") * CG
    core = lax.rem(lax.axis_index("inner"), CORES)
    for copy in smalls:
        copy.wait()

    for row in range(rows):
        blocks = []
        for coarse in range(CG):
            block = None
            for m in range(prolong.shape[1]):
                hit = (prolong_cols[row, m] == first_coarse + coarse) & (m < prolong_count[row])
                term = prolong[row, m] * jnp.where(hit, 1.0, 0.0)
                block = term if block is None else block + term
            blocks.append(block)
        dense[row * size : (row + 1) * size, :] = jnp.concatenate(blocks, axis=1)

    packed = straight_ref.shape[0] - META
    quarter = size // CG
    line = lax.broadcasted_iota(jnp.int32, (META, CG * size), 0)
    lane = lax.broadcasted_iota(jnp.int32, (META, CG * size), 1)
    for cross, ref in enumerate((straight_ref, crossed_ref)):
        row = fetch[core if cross == 0 else 1 - core]
        meta = jnp.zeros((META, CG * size), jnp.float32)
        for m in range(prolong.shape[1]):
            tile = prolong[row, m]
            ref[m * quarter : (m + 1) * quarter, :] = jnp.concatenate(
                [tile[part * quarter : (part + 1) * quarter, :] for part in range(CG)], axis=1
            )
            column = jnp.where(
                m < prolong_count[row], prolong_cols[row, m] - first_coarse, -1
            ).astype(jnp.float32)
            meta = jnp.where((line == cross) & (lane == m), column, meta)
        ref[packed:, :] = meta

    for first in range(0, rows, 2):
        pair = range(first, min(first + 2, rows))
        for row in pair:
            copies[row].wait()
        for entry in range(entries):
            for row in pair:
                slot = jnp.where(entry < count[row], cols[row, entry], rows + 2 * fetched)
                slots[row][slot] += tiles[row, entry]

    def gathered(first, length):
        return jnp.concatenate(
            [
                jnp.concatenate([slots[row][first + j] for j in range(length)], axis=1)
                for row in range(rows)
            ],
            axis=0,
        )

    turned = split(dense[...].T)
    send_outer_ref[...] = product(turned, split(gathered(rows + (1 - core) * fetched, fetched)))
    outer_ref[...] = gathered(rows + core * fetched, fetched)
    local_ref[...] = gathered(0, rows)


def middle_kernel(dense_ref, outer_ref, local_ref, outer_keep_ref, keep_ref, send_ref, whole):
    core = lax.rem(lax.axis_index("inner"), CORES)
    half = keep_ref.shape[0]
    value = dense_ref[...]
    turned = split(value.T)
    outer_keep_ref[...] = product(turned, split(outer_ref[...]))
    applied = product(split(local_ref[...]), split(value))
    whole[...] = product(turned, split(applied))
    for ref, side in ((keep_ref, core), (send_ref, 1 - core)):
        ref[...] = whole[pl.ds(pl.multiple_of(side * half, half), half), :]


def window_kernel(held_ref, came_ref, *refs):
    ghosts, result_ref, prolong = refs[:-2], refs[-2], refs[-1]
    position = lax.axis_index("inner")
    core, chip = lax.rem(position, CORES), lax.div(position, CORES)
    chips = len(ghosts)
    size = result_ref.shape[0] // CG
    quarter = size // CG
    packed = (ghosts[0].shape[0] - META) // CORES
    for shift, ghost in enumerate(ghosts):
        for cross in range(CORES):
            source = lax.rem(shift - chip + chips, chips) * CORES + lax.rem(1 - core + cross, CORES)
            blocks = [None] * CG
            for m in range(packed // quarter):
                first = cross * packed + m * quarter
                column = ghost[CORES * packed + cross : CORES * packed + cross + 1, m : m + 1]
                tile = jnp.concatenate(
                    [
                        ghost[first : first + quarter, part * size : (part + 1) * size]
                        for part in range(CG)
                    ],
                    axis=0,
                )
                for coarse in range(CG):
                    term = tile * jnp.where(column == coarse, 1.0, 0.0)
                    blocks[coarse] = term if m == 0 else blocks[coarse] + term
            prolong[pl.ds(pl.multiple_of(source * size, size), size), :] = jnp.concatenate(
                blocks, axis=1
            )
    result_ref[...] = product(split(held_ref[...] + came_ref[...]), split(prolong[...]))


def store_kernel(places, *refs):
    values, (out_hbm, blocks, sems) = refs[: len(places)], refs[-3:]
    core = lax.rem(lax.axis_index("inner"), CORES)
    size = blocks.shape[-1]
    copies = []
    for value, place in zip(values, places):
        first_row, first_column = place(core)
        for g in range(value.shape[0] // size):
            index = len(copies)
            for h in range(CG):
                blocks[index, h] = value[g * size : (g + 1) * size, h * size : (h + 1) * size]
            copy = pltpu.make_async_copy(
                blocks.at[index],
                out_hbm.at[first_row + g, pl.ds(first_column, CG)],
                sems.at[index],
            )
            copy.start()
            copies.append(copy)
    for copy in copies:
        copy.wait()


def outer_place(core):
    return 0, 2 * CG * core


def middle_place(core):
    return core * (CG // CORES), CG


def other_outer_place(core):
    return outer_place(1 - core)


def other_middle_place(core):
    return middle_place(1 - core)


VMEM = pl.BlockSpec(memory_space=pltpu.VMEM)
HBM = pl.BlockSpec(memory_space=pltpu.HBM)
PARAMS = pltpu.CompilerParams(vmem_limit_bytes=VMEM_BYTES)


def f32(*shape):
    return jax.ShapeDtypeStruct(shape, jnp.float32)


def per_device(
    operator_tiles,
    operator_cols,
    operator_count,
    prolong_tiles,
    prolong_cols,
    prolong_count,
    fetch_rows,
):
    rows, entries, size, _ = operator_tiles.shape
    subs, fetched = lax.axis_size("sub"), lax.axis_size("inner")
    chips = fetched // CORES
    width = CG * size
    half = width // CORES
    packed = prolong_tiles.shape[1] * size // CG

    smem = pltpu.SMEM
    send_outer, outer, local, dense, straight, crossed = pl.pallas_call(
        left_kernel,
        out_shape=[
            f32(width, fetched * size),
            f32(rows * size, fetched * size),
            f32(rows * size, rows * size),
            f32(rows * size, width),
            f32(packed + META, width),
            f32(packed + META, width),
        ],
        in_specs=[HBM] * 7,
        out_specs=[VMEM] * 6,
        scratch_shapes=[
            smem(operator_cols.shape, jnp.int32),
            smem(operator_count.shape, jnp.int32),
            smem(prolong_cols.shape, jnp.int32),
            smem(prolong_count.shape, jnp.int32),
            smem((2,), jnp.int32),
            pltpu.VMEM(operator_tiles.shape, jnp.float32),
            pltpu.VMEM(prolong_tiles.shape, jnp.float32),
        ]
        + [pltpu.VMEM((rows + 2 * fetched + 1, size, size), jnp.float32)] * rows
        + [pltpu.SemaphoreType.DMA((rows,)), pltpu.SemaphoreType.DMA((6,))],
        compiler_params=PARAMS,
        name="left",
    )(
        *(
            pltpu.with_memory_space_constraint(value, pltpu.HBM)
            for value in (
                operator_cols,
                operator_count,
                prolong_cols,
                prolong_count,
                fetch_rows.reshape(-1),
                operator_tiles,
                prolong_tiles,
            )
        )
    )

    keep_outer, keep_inner, send_inner = pl.pallas_call(
        middle_kernel,
        out_shape=[f32(width, fetched * size), f32(half, width), f32(half, width)],
        in_specs=[VMEM] * 3,
        out_specs=[VMEM] * 3,
        scratch_shapes=[pltpu.VMEM((width, width), jnp.float32)],
        compiler_params=PARAMS,
        name="middle",
    )(dense, outer, local)

    swap_cores = [(i, i ^ 1) for i in range(fetched)]

    def other_core(value):
        return lax.ppermute(value, "inner", swap_cores)

    def chip_sum(value):
        step = 1
        while step < chips:
            came = lax.ppermute(
                value, "inner", [(i, i ^ (step * CORES)) for i in range(fetched)]
            )
            step *= 2
            if step < chips:
                value = value + came
        return value, came

    held_outer, came_outer = chip_sum(keep_outer + other_core(send_outer))
    crossed = other_core(crossed)
    edge = jnp.concatenate(
        [straight[:packed], crossed[:packed], straight[packed:] + crossed[packed:]], axis=0
    )
    ghosts = []
    for shift in range(chips):
        pairs = []
        for sub in range(subs - 1):
            for chip in range(chips):
                below = (sub * chips + chip) * CORES + 1
                above = ((sub + 1) * chips + (shift - chip) % chips) * CORES
                pairs += [(below, above), (above, below)]
        first = [CORES * chip for chip in range(chips)]
        last = [subs * fetched - CORES * (chips - chip) + 1 for chip in range(chips)]
        if shift == 0:
            pairs += [*zip(first, last), *zip(last, first)]
        ghosts.append(lax.ppermute(edge, ("sub", "inner"), pairs))

    held_inner, came_inner = chip_sum(keep_inner + other_core(send_inner))

    window = pl.pallas_call(
        window_kernel,
        out_shape=f32(width, width),
        in_specs=[VMEM] * (2 + len(ghosts)),
        out_specs=VMEM,
        scratch_shapes=[pltpu.VMEM((fetched * size, width), jnp.float32)],
        compiler_params=PARAMS,
        name="window",
    )(held_outer, came_outer, *ghosts)

    def store(name, places, values, out=()):
        rows_stored = sum(value.shape[0] for value in values) // size
        return (
            pl.pallas_call(
                functools.partial(store_kernel, places),
                out_shape=f32(CG, 3 * CG, size, size),
                in_specs=[VMEM] * len(values) + [HBM] * len(out),
                out_specs=HBM,
                scratch_shapes=[
                    pltpu.VMEM((rows_stored, CG, size, size), jnp.float32),
                    pltpu.SemaphoreType.DMA((rows_stored,)),
                ],
                input_output_aliases={len(values): 0} if out else {},
                compiler_params=PARAMS,
                name=name,
            )(*values, *out),
        )

    out = store("store_own", (outer_place,), (window,))
    came_inner, *out = lax.optimization_barrier((came_inner, *out))
    middle = held_inner + came_inner
    out = store(
        "store_both", (other_outer_place, middle_place), (other_core(window), middle), out
    )
    return store("store_other", (other_middle_place,), (other_core(middle),), out)[0]


def solution(mesh):
    placed = (
        P(("sub", "inner"), None, None, None),
        P(("sub", "inner"), None),
        P(("sub", "inner")),
        P(("sub", "inner"), None, None, None),
        P(("sub", "inner"), None),
        P(("sub", "inner")),
        P(("sub", "inner"), None),
    )
    return jax.shard_map(
        per_device,
        mesh=mesh,
        in_specs=placed,
        out_specs=P("sub", None, None, None),
        check_vma=False,
    )
```

```python
import functools

import jax
import jax.numpy as jnp
from jax import lax
from jax.experimental import pallas as pl
from jax.experimental.pallas import tpu as pltpu
from jax.sharding import PartitionSpec as P

CG = 4
CORES = 2
META = 8
TOGETHER = 2
VMEM_BYTES = 32 * 1024 * 1024


def split(value):
    high = value.astype(jnp.bfloat16)
    low = (value - high.astype(jnp.float32)).astype(jnp.bfloat16)
    return high, low


def product(left, right):
    dot = functools.partial(jnp.dot, preferred_element_type=jnp.float32)
    return dot(left[0], right[0]) + (dot(left[1], right[0]) + dot(left[0], right[1]))


def side_of(position):
    return lax.rem(position + lax.div(position, CORES), CORES)


def device_of(chip, side):
    return chip * CORES + (side + chip) % CORES


def left_kernel(
    cols_hbm,
    count_hbm,
    prolong_cols_hbm,
    prolong_count_hbm,
    fetch_hbm,
    tiles_hbm,
    prolong_hbm,
    send_outer_ref,
    outer_ref,
    local_ref,
    dense,
    straight_ref,
    crossed_ref,
    cols,
    count,
    prolong_cols,
    prolong_count,
    fetch,
    tiles,
    prolong,
    *rest,
):
    slots, (tile_sems, small_sems) = rest[:-2], rest[-2:]
    rows, entries, size, _ = tiles.shape
    fetched = outer_ref.shape[1] // size
    smalls = [
        pltpu.make_async_copy(source, target, small_sems.at[index])
        for index, (source, target) in enumerate(
            (
                (prolong_cols_hbm, prolong_cols),
                (prolong_count_hbm, prolong_count),
                (fetch_hbm, fetch),
                (cols_hbm, cols),
                (count_hbm, count),
                (prolong_hbm, prolong),
            )
        )
    ]
    copies = [
        pltpu.make_async_copy(
            tiles_hbm.at[pl.ds(first, TOGETHER)],
            tiles.at[pl.ds(first, TOGETHER)],
            tile_sems.at[first // TOGETHER],
        )
        for first in range(0, rows, TOGETHER)
    ]
    for copy in smalls + copies:
        copy.start()
    for ref in slots:
        ref[...] = jnp.zeros_like(ref)
    first_coarse = lax.axis_index("sub") * CG
    side = side_of(lax.axis_index("inner"))
    for copy in smalls:
        copy.wait()

    for row in range(rows):
        blocks = []
        for coarse in range(CG):
            block = None
            for m in range(prolong.shape[1]):
                hit = (prolong_cols[row, m] == first_coarse + coarse) & (m < prolong_count[row])
                term = prolong[row, m] * jnp.where(hit, 1.0, 0.0)
                block = term if block is None else block + term
            blocks.append(block)
        dense[row * size : (row + 1) * size, :] = jnp.concatenate(blocks, axis=1)

    packed = straight_ref.shape[0] - META
    quarter = size // CG
    line = lax.broadcasted_iota(jnp.int32, (META, CG * size), 0)
    lane = lax.broadcasted_iota(jnp.int32, (META, CG * size), 1)
    for cross, ref in enumerate((straight_ref, crossed_ref)):
        row = fetch[side if cross == 0 else 1 - side]
        meta = jnp.zeros((META, CG * size), jnp.float32)
        for m in range(prolong.shape[1]):
            tile = prolong[row, m]
            ref[m * quarter : (m + 1) * quarter, :] = jnp.concatenate(
                [tile[part * quarter : (part + 1) * quarter, :] for part in range(CG)], axis=1
            )
            column = jnp.where(
                m < prolong_count[row], prolong_cols[row, m] - first_coarse, -1
            ).astype(jnp.float32)
            meta = jnp.where((line == cross) & (lane == m), column, meta)
        ref[packed:, :] = meta

    for copy, first in zip(copies, range(0, rows, TOGETHER)):
        pair = range(first, first + TOGETHER)
        copy.wait()
        for entry in range(entries):
            for row in pair:
                slot = jnp.where(entry < count[row], cols[row, entry], rows + 2 * fetched)
                slots[row][slot] += tiles[row, entry]

    def gathered(first, length):
        return jnp.concatenate(
            [
                jnp.concatenate([slots[row][first + j] for j in range(length)], axis=1)
                for row in range(rows)
            ],
            axis=0,
        )

    turned = split(dense[...].T)
    send_outer_ref[...] = product(turned, split(gathered(rows + (1 - side) * fetched, fetched)))
    outer_ref[...] = gathered(rows + side * fetched, fetched)
    local_ref[...] = gathered(0, rows)


def middle_kernel(dense_ref, outer_ref, local_ref, outer_keep_ref, keep_ref, send_ref, whole):
    side = side_of(lax.axis_index("inner"))
    half = keep_ref.shape[0]
    value = dense_ref[...]
    turned = split(value.T)
    outer_keep_ref[...] = product(turned, split(outer_ref[...]))
    applied = product(split(local_ref[...]), split(value))
    whole[...] = product(turned, split(applied))
    for ref, owner in ((keep_ref, side), (send_ref, 1 - side)):
        ref[...] = whole[pl.ds(pl.multiple_of(owner * half, half), half), :]


def window_kernel(held_ref, came_ref, *refs):
    ghosts, result_ref, prolong = refs[:-2], refs[-2], refs[-1]
    position = lax.axis_index("inner")
    side, chip = side_of(position), lax.div(position, CORES)
    chips = len(ghosts)
    size = result_ref.shape[0] // CG
    quarter = size // CG
    packed = (ghosts[0].shape[0] - META) // CORES
    for shift, ghost in enumerate(ghosts):
        for cross in range(CORES):
            there = lax.rem(shift - chip + chips, chips)
            source = there * CORES + lax.rem(1 - side + there + cross, CORES)
            blocks = [None] * CG
            for m in range(packed // quarter):
                first = cross * packed + m * quarter
                column = ghost[CORES * packed + cross : CORES * packed + cross + 1, m : m + 1]
                tile = jnp.concatenate(
                    [
                        ghost[first : first + quarter, part * size : (part + 1) * size]
                        for part in range(CG)
                    ],
                    axis=0,
                )
                for coarse in range(CG):
                    term = tile * jnp.where(column == coarse, 1.0, 0.0)
                    blocks[coarse] = term if m == 0 else blocks[coarse] + term
            prolong[pl.ds(pl.multiple_of(source * size, size), size), :] = jnp.concatenate(
                blocks, axis=1
            )
    result_ref[...] = product(split(held_ref[...] + came_ref[...]), split(prolong[...]))


def store_kernel(places, *refs):
    values, (out_hbm, blocks, sems) = refs[: len(places)], refs[-3:]
    side = side_of(lax.axis_index("inner"))
    size = blocks.shape[-1]
    copies = []
    for value, place in zip(values, places):
        first_row, first_column = place(side)
        for g in range(value.shape[0] // size):
            index = len(copies)
            for h in range(CG):
                blocks[index, h] = value[g * size : (g + 1) * size, h * size : (h + 1) * size]
            copy = pltpu.make_async_copy(
                blocks.at[index],
                out_hbm.at[first_row + g, pl.ds(first_column, CG)],
                sems.at[index],
            )
            copy.start()
            copies.append(copy)
    for copy in copies:
        copy.wait()


def outer_place(side):
    return 0, 2 * CG * side


def middle_place(side):
    return side * (CG // CORES), CG


def other_outer_place(side):
    return outer_place(1 - side)


def other_middle_place(side):
    return middle_place(1 - side)


VMEM = pl.BlockSpec(memory_space=pltpu.VMEM)
HBM = pl.BlockSpec(memory_space=pltpu.HBM)
PARAMS = pltpu.CompilerParams(vmem_limit_bytes=VMEM_BYTES)


def f32(*shape):
    return jax.ShapeDtypeStruct(shape, jnp.float32)


def per_device(
    operator_tiles,
    operator_cols,
    operator_count,
    prolong_tiles,
    prolong_cols,
    prolong_count,
    fetch_rows,
):
    rows, entries, size, _ = operator_tiles.shape
    subs, fetched = lax.axis_size("sub"), lax.axis_size("inner")
    chips = fetched // CORES
    width = CG * size
    half = width // CORES
    packed = prolong_tiles.shape[1] * size // CG

    smem = pltpu.SMEM
    send_outer, outer, local, dense, straight, crossed = pl.pallas_call(
        left_kernel,
        out_shape=[
            f32(width, fetched * size),
            f32(rows * size, fetched * size),
            f32(rows * size, rows * size),
            f32(rows * size, width),
            f32(packed + META, width),
            f32(packed + META, width),
        ],
        in_specs=[HBM] * 7,
        out_specs=[VMEM] * 6,
        scratch_shapes=[
            smem(operator_cols.shape, jnp.int32),
            smem(operator_count.shape, jnp.int32),
            smem(prolong_cols.shape, jnp.int32),
            smem(prolong_count.shape, jnp.int32),
            smem((2,), jnp.int32),
            pltpu.VMEM(operator_tiles.shape, jnp.float32),
            pltpu.VMEM(prolong_tiles.shape, jnp.float32),
        ]
        + [pltpu.VMEM((rows + 2 * fetched + 1, size, size), jnp.float32)] * rows
        + [pltpu.SemaphoreType.DMA((rows,)), pltpu.SemaphoreType.DMA((6,))],
        compiler_params=PARAMS,
        name="left",
    )(
        *(
            pltpu.with_memory_space_constraint(value, pltpu.HBM)
            for value in (
                operator_cols,
                operator_count,
                prolong_cols,
                prolong_count,
                fetch_rows.reshape(-1),
                operator_tiles,
                prolong_tiles,
            )
        )
    )

    keep_outer, keep_inner, send_inner = pl.pallas_call(
        middle_kernel,
        out_shape=[f32(width, fetched * size), f32(half, width), f32(half, width)],
        in_specs=[VMEM] * 3,
        out_specs=[VMEM] * 3,
        scratch_shapes=[pltpu.VMEM((width, width), jnp.float32)],
        compiler_params=PARAMS,
        name="middle",
    )(dense, outer, local)

    swap_cores = [(i, i ^ 1) for i in range(fetched)]

    def other_core(value):
        return lax.ppermute(value, "inner", swap_cores)

    def chip_sum(value):
        step = 1
        while step < chips:
            pairs = [
                (device_of(chip, side), device_of(chip ^ step, side))
                for chip in range(chips)
                for side in range(CORES)
            ]
            came = lax.ppermute(value, "inner", pairs)
            step *= 2
            if step < chips:
                value = value + came
        return value, came

    held_outer, came_outer = chip_sum(keep_outer + other_core(send_outer))
    crossed = other_core(crossed)
    edge = jnp.concatenate(
        [straight[:packed], crossed[:packed], straight[packed:] + crossed[packed:]], axis=0
    )
    ghosts = []
    for shift in range(chips):
        pairs = []
        for sub in range(subs - 1):
            for chip in range(chips):
                below = sub * fetched + device_of(chip, 1)
                above = (sub + 1) * fetched + device_of((shift - chip) % chips, 0)
                pairs += [(below, above), (above, below)]
        first = [device_of(chip, 0) for chip in range(chips)]
        last = [(subs - 1) * fetched + device_of(chip, 1) for chip in range(chips)]
        if shift == 0:
            pairs += [*zip(first, last), *zip(last, first)]
        ghosts.append(lax.ppermute(edge, ("sub", "inner"), pairs))

    held_inner, came_inner = chip_sum(keep_inner + other_core(send_inner))

    window = pl.pallas_call(
        window_kernel,
        out_shape=f32(width, width),
        in_specs=[VMEM] * (2 + len(ghosts)),
        out_specs=VMEM,
        scratch_shapes=[pltpu.VMEM((fetched * size, width), jnp.float32)],
        compiler_params=PARAMS,
        name="window",
    )(held_outer, came_outer, *ghosts)

    def store(name, places, values, out=()):
        rows_stored = sum(value.shape[0] for value in values) // size
        return (
            pl.pallas_call(
                functools.partial(store_kernel, places),
                out_shape=f32(CG, 3 * CG, size, size),
                in_specs=[VMEM] * len(values) + [HBM] * len(out),
                out_specs=HBM,
                scratch_shapes=[
                    pltpu.VMEM((rows_stored, CG, size, size), jnp.float32),
                    pltpu.SemaphoreType.DMA((rows_stored,)),
                ],
                input_output_aliases={len(values): 0} if out else {},
                compiler_params=PARAMS,
                name=name,
            )(*values, *out),
        )

    out = store("store_own", (outer_place,), (window,))
    came_inner, *out = lax.optimization_barrier((came_inner, *out))
    middle = held_inner + came_inner
    out = store(
        "store_both", (other_outer_place, middle_place), (other_core(window), middle), out
    )
    return store("store_other", (other_middle_place,), (other_core(middle),), out)[0]


def solution(mesh):
    placed = (
        P(("sub", "inner"), None, None, None),
        P(("sub", "inner"), None),
        P(("sub", "inner")),
        P(("sub", "inner"), None, None, None),
        P(("sub", "inner"), None),
        P(("sub", "inner")),
        P(("sub", "inner"), None),
    )
    return jax.shard_map(
        per_device,
        mesh=mesh,
        in_specs=placed,
        out_specs=P("sub", None, None, None),
        check_vma=False,
    )
```

```python
import functools

import jax
import jax.numpy as jnp
from jax import lax
from jax.experimental import pallas as pl
from jax.experimental.pallas import tpu as pltpu
from jax.sharding import PartitionSpec as P

CG = 4
CORES = 2
META = 8
TOGETHER = 2
VMEM_BYTES = 32 * 1024 * 1024


def split(value):
    high = value.astype(jnp.bfloat16)
    low = (value - high.astype(jnp.float32)).astype(jnp.bfloat16)
    return high, low


def product(left, right):
    dot = functools.partial(jnp.dot, preferred_element_type=jnp.float32)
    return dot(left[0], right[0]) + (dot(left[1], right[0]) + dot(left[0], right[1]))


def side_of(position):
    return lax.rem(position + lax.div(position, CORES), CORES)


def device_of(chip, side):
    return chip * CORES + (side + chip) % CORES


def left_kernel(
    cols_hbm,
    count_hbm,
    prolong_cols_hbm,
    prolong_count_hbm,
    fetch_hbm,
    tiles_hbm,
    prolong_hbm,
    send_outer_ref,
    outer_ref,
    local_ref,
    dense,
    straight_ref,
    crossed_ref,
    cols,
    count,
    prolong_cols,
    prolong_count,
    fetch,
    tiles,
    prolong,
    *rest,
):
    slots, (tile_sems, small_sems) = rest[:-2], rest[-2:]
    rows, entries, size, _ = tiles.shape
    fetched = outer_ref.shape[1] // size
    smalls = [
        pltpu.make_async_copy(source, target, small_sems.at[index])
        for index, (source, target) in enumerate(
            (
                (prolong_cols_hbm, prolong_cols),
                (prolong_count_hbm, prolong_count),
                (fetch_hbm, fetch),
                (cols_hbm, cols),
                (count_hbm, count),
                (prolong_hbm, prolong),
            )
        )
    ]
    copies = [
        pltpu.make_async_copy(
            tiles_hbm.at[pl.ds(first, TOGETHER)],
            tiles.at[pl.ds(first, TOGETHER)],
            tile_sems.at[first // TOGETHER],
        )
        for first in range(0, rows, TOGETHER)
    ]
    for copy in smalls + copies:
        copy.start()
    for ref in slots:
        ref[...] = jnp.zeros_like(ref)
    first_coarse = lax.axis_index("sub") * CG
    side = side_of(lax.axis_index("inner"))
    for copy in smalls:
        copy.wait()

    for row in range(rows):
        blocks = []
        for coarse in range(CG):
            block = None
            for m in range(prolong.shape[1]):
                hit = (prolong_cols[row, m] == first_coarse + coarse) & (m < prolong_count[row])
                term = prolong[row, m] * jnp.where(hit, 1.0, 0.0)
                block = term if block is None else block + term
            blocks.append(block)
        dense[row * size : (row + 1) * size, :] = jnp.concatenate(blocks, axis=1)

    packed = straight_ref.shape[0] - META
    quarter = size // CG
    line = lax.broadcasted_iota(jnp.int32, (META, CG * size), 0)
    lane = lax.broadcasted_iota(jnp.int32, (META, CG * size), 1)
    for cross, ref in enumerate((straight_ref, crossed_ref)):
        row = fetch[side if cross == 0 else 1 - side]
        meta = jnp.zeros((META, CG * size), jnp.float32)
        for m in range(prolong.shape[1]):
            tile = prolong[row, m]
            ref[m * quarter : (m + 1) * quarter, :] = jnp.concatenate(
                [tile[part * quarter : (part + 1) * quarter, :] for part in range(CG)], axis=1
            )
            column = jnp.where(
                m < prolong_count[row], prolong_cols[row, m] - first_coarse, -1
            ).astype(jnp.float32)
            meta = jnp.where((line == cross) & (lane == m), column, meta)
        ref[packed:, :] = meta

    for copy, first in zip(copies, range(0, rows, TOGETHER)):
        pair = range(first, first + TOGETHER)
        copy.wait()
        for entry in range(entries):
            for row in pair:
                slot = jnp.where(entry < count[row], cols[row, entry], rows + 2 * fetched)
                slots[row][slot] += tiles[row, entry]

    def gathered(first, length):
        return jnp.concatenate(
            [
                jnp.concatenate([slots[row][first + j] for j in range(length)], axis=1)
                for row in range(rows)
            ],
            axis=0,
        )

    turned = split(dense[...].T)
    send_outer_ref[...] = product(turned, split(gathered(rows + (1 - side) * fetched, fetched)))
    outer_ref[...] = gathered(rows + side * fetched, fetched)
    local_ref[...] = gathered(0, rows)


def middle_kernel(dense_ref, outer_ref, local_ref, outer_keep_ref, keep_ref, send_ref, whole):
    side = side_of(lax.axis_index("inner"))
    half = keep_ref.shape[0]
    value = dense_ref[...]
    turned = split(value.T)
    outer_keep_ref[...] = product(turned, split(outer_ref[...]))
    applied = product(split(local_ref[...]), split(value))
    whole[...] = product(turned, split(applied))
    for ref, owner in ((keep_ref, side), (send_ref, 1 - side)):
        ref[...] = whole[pl.ds(pl.multiple_of(owner * half, half), half), :]


def window_kernel(held_ref, came_ref, *refs):
    ghosts, result_ref, prolong = refs[:-2], refs[-2], refs[-1]
    position = lax.axis_index("inner")
    side, chip = side_of(position), lax.div(position, CORES)
    chips = len(ghosts)
    size = result_ref.shape[0] // CG
    quarter = size // CG
    packed = (ghosts[0].shape[0] - META) // CORES
    for shift, ghost in enumerate(ghosts):
        for cross in range(CORES):
            there = lax.rem(shift - chip + chips, chips)
            source = there * CORES + lax.rem(1 - side + there + cross, CORES)
            blocks = [None] * CG
            for m in range(packed // quarter):
                first = cross * packed + m * quarter
                column = ghost[CORES * packed + cross : CORES * packed + cross + 1, m : m + 1]
                tile = jnp.concatenate(
                    [
                        ghost[first : first + quarter, part * size : (part + 1) * size]
                        for part in range(CG)
                    ],
                    axis=0,
                )
                for coarse in range(CG):
                    term = tile * jnp.where(column == coarse, 1.0, 0.0)
                    blocks[coarse] = term if m == 0 else blocks[coarse] + term
            prolong[pl.ds(pl.multiple_of(source * size, size), size), :] = jnp.concatenate(
                blocks, axis=1
            )
    result_ref[...] = product(split(held_ref[...] + came_ref[...]), split(prolong[...]))


def store_kernel(places, *refs):
    values, (out_hbm, blocks, sems) = refs[: len(places)], refs[-3:]
    side = side_of(lax.axis_index("inner"))
    size = blocks.shape[-1]
    copies = []
    for value, place in zip(values, places):
        first_row, first_column = place(side)
        for g in range(value.shape[0] // size):
            index = len(copies)
            for h in range(CG):
                blocks[index, h] = value[g * size : (g + 1) * size, h * size : (h + 1) * size]
            copy = pltpu.make_async_copy(
                blocks.at[index],
                out_hbm.at[first_row + g, pl.ds(first_column, CG)],
                sems.at[index],
            )
            copy.start()
            copies.append(copy)
    for copy in copies:
        copy.wait()


def outer_place(side):
    return 0, 2 * CG * side


def middle_place(side):
    return side * (CG // CORES), CG


def other_outer_place(side):
    return outer_place(1 - side)


def other_middle_place(side):
    return middle_place(1 - side)


VMEM = pl.BlockSpec(memory_space=pltpu.VMEM)
HBM = pl.BlockSpec(memory_space=pltpu.HBM)
PARAMS = pltpu.CompilerParams(vmem_limit_bytes=VMEM_BYTES)


def f32(*shape):
    return jax.ShapeDtypeStruct(shape, jnp.float32)


def per_device(
    operator_tiles,
    operator_cols,
    operator_count,
    prolong_tiles,
    prolong_cols,
    prolong_count,
    fetch_rows,
):
    rows, entries, size, _ = operator_tiles.shape
    subs, fetched = lax.axis_size("sub"), lax.axis_size("inner")
    chips = fetched // CORES
    width = CG * size
    half = width // CORES
    packed = prolong_tiles.shape[1] * size // CG

    smem = pltpu.SMEM
    send_outer, outer, local, dense, straight, crossed = pl.pallas_call(
        left_kernel,
        out_shape=[
            f32(width, fetched * size),
            f32(rows * size, fetched * size),
            f32(rows * size, rows * size),
            f32(rows * size, width),
            f32(packed + META, width),
            f32(packed + META, width),
        ],
        in_specs=[HBM] * 7,
        out_specs=[VMEM] * 6,
        scratch_shapes=[
            smem(operator_cols.shape, jnp.int32),
            smem(operator_count.shape, jnp.int32),
            smem(prolong_cols.shape, jnp.int32),
            smem(prolong_count.shape, jnp.int32),
            smem((2,), jnp.int32),
            pltpu.VMEM(operator_tiles.shape, jnp.float32),
            pltpu.VMEM(prolong_tiles.shape, jnp.float32),
        ]
        + [pltpu.VMEM((rows + 2 * fetched + 1, size, size), jnp.float32)] * rows
        + [pltpu.SemaphoreType.DMA((rows,)), pltpu.SemaphoreType.DMA((6,))],
        compiler_params=PARAMS,
        name="left",
    )(
        *(
            pltpu.with_memory_space_constraint(value, pltpu.HBM)
            for value in (
                operator_cols,
                operator_count,
                prolong_cols,
                prolong_count,
                fetch_rows.reshape(-1),
                operator_tiles,
                prolong_tiles,
            )
        )
    )

    keep_outer, keep_inner, send_inner = pl.pallas_call(
        middle_kernel,
        out_shape=[f32(width, fetched * size), f32(half, width), f32(half, width)],
        in_specs=[VMEM] * 3,
        out_specs=[VMEM] * 3,
        scratch_shapes=[pltpu.VMEM((width, width), jnp.float32)],
        compiler_params=PARAMS,
        name="middle",
    )(dense, outer, local)

    swap_cores = [(i, i ^ 1) for i in range(fetched)]

    def other_core(value):
        return lax.ppermute(value, "inner", swap_cores)

    def chip_sum(value):
        step = 1
        while step < chips:
            pairs = [
                (device_of(chip, side), device_of(chip ^ step, side))
                for chip in range(chips)
                for side in range(CORES)
            ]
            came = lax.ppermute(value, "inner", pairs)
            step *= 2
            if step < chips:
                value = value + came
        return value, came

    held_outer, came_outer = chip_sum(keep_outer + other_core(send_outer))
    crossed = other_core(crossed)
    edge = jnp.concatenate(
        [straight[:packed], crossed[:packed], straight[packed:] + crossed[packed:]], axis=0
    )
    ghosts = []
    for shift in range(chips):
        pairs = []
        for sub in range(subs - 1):
            for chip in range(chips):
                below = sub * fetched + device_of(chip, 1)
                above = (sub + 1) * fetched + device_of((shift - chip) % chips, 0)
                pairs += [(below, above), (above, below)]
        first = [device_of(chip, 0) for chip in range(chips)]
        last = [(subs - 1) * fetched + device_of(chip, 1) for chip in range(chips)]
        if shift > 0:
            pairs += [*zip(first, last), *zip(last, first)]
        ghosts.append(lax.ppermute(edge, ("sub", "inner"), pairs))

    send_inner, held_outer = lax.optimization_barrier((send_inner, held_outer))
    held_inner, came_inner = chip_sum(keep_inner + other_core(send_inner))

    window = pl.pallas_call(
        window_kernel,
        out_shape=f32(width, width),
        in_specs=[VMEM] * (2 + len(ghosts)),
        out_specs=VMEM,
        scratch_shapes=[pltpu.VMEM((fetched * size, width), jnp.float32)],
        compiler_params=PARAMS,
        name="window",
    )(held_outer, came_outer, *ghosts)

    def store(name, places, values, out=()):
        rows_stored = sum(value.shape[0] for value in values) // size
        return (
            pl.pallas_call(
                functools.partial(store_kernel, places),
                out_shape=f32(CG, 3 * CG, size, size),
                in_specs=[VMEM] * len(values) + [HBM] * len(out),
                out_specs=HBM,
                scratch_shapes=[
                    pltpu.VMEM((rows_stored, CG, size, size), jnp.float32),
                    pltpu.SemaphoreType.DMA((rows_stored,)),
                ],
                input_output_aliases={len(values): 0} if out else {},
                compiler_params=PARAMS,
                name=name,
            )(*values, *out),
        )

    out = store("store_own", (outer_place,), (window,))
    came_inner, *out = lax.optimization_barrier((came_inner, *out))
    middle = held_inner + came_inner
    out = store(
        "store_both", (other_outer_place, middle_place), (other_core(window), middle), out
    )
    return store("store_other", (other_middle_place,), (other_core(middle),), out)[0]


def solution(mesh):
    placed = (
        P(("sub", "inner"), None, None, None),
        P(("sub", "inner"), None),
        P(("sub", "inner")),
        P(("sub", "inner"), None, None, None),
        P(("sub", "inner"), None),
        P(("sub", "inner")),
        P(("sub", "inner"), None),
    )
    return jax.shard_map(
        per_device,
        mesh=mesh,
        in_specs=placed,
        out_specs=P("sub", None, None, None),
        check_vma=False,
    )
```
